128 devices in a mesh: dp: 2 (over core), vocab: 64 (over z, y, x).
Axes of the slice: x: 4, y: 4, z: 4, core: 2. Of those that a mesh axis runs over, the one named last changes fastest.
Arguments:
- hidden: bfloat16 [384, 8192], P('dp', 'vocab'), may hold values from -12 to 12
- tangent_hidden: bfloat16 [384, 8192], P('dp', 'vocab'), may hold values from -6 to 6
- head: bfloat16 [8192, 65536], P('dp', 'vocab'), may hold values from -1 to 1
- tangent_head: bfloat16 [8192, 65536], P('dp', 'vocab'), may hold values from -0.0625 to 0.0625
- allowed: int32 [384, 512], P('dp', 'vocab'), may hold values from 0 to 1, as said below
Outputs:
- head_product: bfloat16 [8192, 65536], P('dp', 'vocab')
- hidden_product: bfloat16 [384, 8192], P('dp', 'vocab')
The draws below stay inside these ranges and needn't reach their ends.
Inputs may be any that keep to these rules, and one draw needn't show every extreme that they name: Every token allows block 0. The chance that a block is allowed rises along the vocabulary from about a tenth to about nine tenths.
All inputs are finite; a program needn't handle non-finite values.
Results may differ from the reference program's by a relative error of at most 0.012.
Values may be sent and summed in bfloat16 or wider, within the bound.
No kernel may reach another device: no remote copies, remote signals or barrier semaphores. Data moves between devices by JAX's collectives and lax.ppermute only.
A program may use at most 192 MiB of HBM per device.

```python
import math
import jax
import jax.numpy as jnp
from jax import lax

D = 8192
VOC_DEV = 1024
TOK_DEV = 192
TOKENS = 384
VOCAB = 65536
NBLK = 512
N_DP = 2
N_VOCAB = 64


def shared_direction(key):
    return jax.random.normal(jax.random.fold_in(key, 500), (D,), jnp.float32)


def draw_head(key, part):
    direction = shared_direction(key)
    key = jax.random.fold_in(key, 11)
    spread = 3.0 / math.sqrt(D)
    values = jnp.clip(jax.random.normal(key, (D, VOCAB), jnp.float32), -6.0, 6.0) * spread
    values = values.at[:, 0].set(direction * spread)
    values = values.at[:, 1].set(direction * (0.993 * spread))
    return jnp.clip(values, -1.0, 1.0).astype(jnp.bfloat16)


def draw_hidden(key, part):
    key = jax.random.fold_in(key, 12)
    values = jnp.clip(jax.random.normal(key, (TOKENS, D), jnp.float32), -6.0, 6.0)
    return jnp.clip(values, -12.0, 12.0).astype(jnp.bfloat16)


def draw_allowed(key, part):
    key = jax.random.fold_in(key, 13)
    ticket = jax.random.randint(key, (TOKENS, NBLK), 0, 1000)
    blocks = jnp.arange(NBLK)[None, :]
    limit = 100 + 800 * blocks // NBLK
    chosen = (ticket < limit).astype(jnp.int32)
    return chosen.at[:, 0].set(1)


def shard_levels(key, shape, pieces, low, top_value):
    loudness, own = 1.0, jax.random.fold_in(key, 6)
    for axis_at, blocks in pieces:
        draws = jnp.exp(jax.random.uniform(jax.random.fold_in(own, axis_at), (blocks,), jnp.float32, low / len(pieces), top_value / len(pieces)))
        loudness = loudness * jnp.repeat(draws, shape[axis_at] // blocks).reshape([-1 if axis == axis_at else 1 for axis in range(len(shape))])
    return loudness


def scatter_about(stream_key, extent, scale, most, cuts=(), kind=jnp.bfloat16):
    array = jax.random.normal(stream_key, extent, jnp.float32) * scale
    if len(cuts) > 0:
        array = shard_levels(stream_key, extent, cuts, -0.22, 0.18) * array
    return jnp.clip(array, min=-most, max=most).astype(kind)


def setup_inputs(seed: int = 0) -> dict:
    streams_of = jax.random.split(jax.random.key(seed), 6)
    return {
        "hidden": draw_hidden(jax.random.fold_in(streams_of[5], 71), 0),
        "tangent_hidden": scatter_about(streams_of[1], (TOKENS, D), 1.0, 6.0, ((0, 2), (1, 64))),
        "head": draw_head(jax.random.fold_in(streams_of[5], 71), 0),
        "tangent_head": scatter_about(streams_of[3], (D, VOCAB), D ** -0.5, 0.0625, ((0, 2), (1, 64))),
        "allowed": draw_allowed(jax.random.fold_in(streams_of[5], 71), 0),
    }


def reference(hidden, tangent_hidden, head, tangent_head, allowed):
    logits = jnp.dot(hidden, head, preferred_element_type=jnp.float32)
    tangent = jnp.dot(tangent_hidden, head, preferred_element_type=jnp.float32) + jnp.dot(hidden, tangent_head, preferred_element_type=jnp.float32)
    allowed_cols = jnp.repeat(allowed > 0, 128, axis=1)
    top_logit = jnp.max(jnp.where(allowed_cols, logits, -jnp.inf), axis=1)
    weights = jnp.exp(jnp.where(allowed_cols, logits - top_logit[:, None], -jnp.inf))
    denominator = jnp.sum(weights, axis=1)
    moment = jnp.sum(weights * tangent, axis=1)
    product = (weights / denominator[:, None] * (tangent - (moment / denominator)[:, None])).astype(jnp.bfloat16)

    def head_block(index):
        start = (index * VOC_DEV).astype(jnp.int32)
        block = lax.dynamic_slice_in_dim(product, start, VOC_DEV, 1)
        summed = jnp.zeros((D, VOC_DEV), jnp.float32)
        for group in range(N_DP):
            rows_in = hidden[group * TOK_DEV:(group + 1) * TOK_DEV]
            block_rows = block[group * TOK_DEV:(group + 1) * TOK_DEV]
            partial_term = lax.dot_general(rows_in, block_rows, (((0,), (0,)), ((), ())), preferred_element_type=jnp.float32)
            summed = summed + partial_term.astype(jnp.bfloat16).astype(jnp.float32)
        return summed.astype(jnp.bfloat16)

    stacked = lax.map(head_block, jnp.arange(N_VOCAB, dtype=jnp.int32))
    head_product = jnp.transpose(stacked, (1, 0, 2)).reshape(D, VOCAB)
    hidden_product = lax.dot_general(product, head, (((1,), (1,)), ((), ())), preferred_element_type=jnp.float32).astype(jnp.bfloat16)
    return head_product, hidden_product
```

```python
import functools

import jax
import jax.numpy as jnp
from jax import lax
from jax.experimental import pallas as pl
from jax.experimental.pallas import tpu as pltpu
from jax.sharding import PartitionSpec as P

AXES = ("dp", "vocab")
SIDE = 4
TOK = 192
COLS = 1024
NEG = -1e30
VMEM = 48 * 1024 * 1024
F32 = jnp.float32
BF16 = jnp.bfloat16


def flat(k, z, y, x):
    return k * 64 + (z % 4) * 16 + (y % 4) * 4 + x % 4


def sites():
    return [(k, z, y, x) for k in range(2) for z in range(4) for y in range(4) for x in range(4)]


def shift(own, d):
    pairs = []
    for k, z, y, x in sites():
        along_x = (k == 0) == own
        target = flat(k, z, y, x + d) if along_x else flat(k, z, y + d, x)
        pairs.append((flat(k, z, y, x), target))
    return pairs


def swap_pairs():
    return [(flat(k, z, y, x), flat(1 - k, z, y, x)) for k, z, y, x in sites()]


def depth_groups():
    return [[flat(k, r + 2 * k, y, x) for r in range(4)] for k in range(2) for y in range(4) for x in range(4)]


def middle_groups():
    return [[flat(0, z, m, x) for m in range(4)] for z in range(4) for x in range(4)] + [
        [flat(1, z, y, m) for m in range(4)] for z in range(4) for y in range(4)
    ]


def plane_groups():
    return [[flat(0, r, m, x) for m in range(4) for r in range(4)] for x in range(4)] + [
        [flat(1, r + 2, y, m) for m in range(4) for r in range(4)] for y in range(4)
    ]


def permute(value, pairs):
    return lax.ppermute(value, AXES, pairs)


def exchange(value, groups):
    return lax.all_to_all(value, AXES, split_axis=0, concat_axis=0, tiled=True, axis_index_groups=groups)


def spread(value, groups):
    size = len(groups[0])
    return exchange(jnp.broadcast_to(value[None], (size,) + value.shape), groups)


def score_kernel(tab, *refs, own):
    chunks, heads, theads = refs[:4], refs[4:8], refs[8:12]
    i = pl.program_id(0)
    if own:
        got, allowed, weights, tangent, stats, acc, left = refs[12:]
    else:
        acc, left = refs[12:]

    @pl.when(i == 0)
    def _():
        acc[...] = jnp.zeros_like(acc)

    for d in range(4):

        @pl.when(i // 2 == d)
        def _():
            for j in range(2):
                for q in range(2):
                    at = 128 * (2 * j + q)
                    left[:, at : at + 128] = chunks[d][j, q]

    for n in range(4):
        cols = slice(256 * n, 256 * n + 256)
        right = jnp.concatenate([h[:, cols] for h in heads], axis=0)
        turn = jnp.concatenate([h[:, cols] for h in theads], axis=0)
        both = jnp.dot(left[...], right, preferred_element_type=F32)
        more = jnp.dot(left[:TOK], turn, preferred_element_type=F32)
        acc[:TOK, cols] += both[:TOK]
        acc[TOK:, cols] += both[TOK:] + more

    if own:

        @pl.when(i == 7)
        def _():
            lane = lax.broadcasted_iota(jnp.int32, (32, 128), 1)
            parts = []
            for r in range(0, TOK, 32):
                rows, trows = slice(r, r + 32), slice(TOK + r, TOK + r + 32)
                logit = acc[rows, :] + got[rows, :]
                tang = acc[trows, :] + got[trows, :]
                ok = jnp.concatenate(
                    [jnp.broadcast_to(allowed[rows, b : b + 1], (32, 128)) for b in range(8)], axis=1
                ) > 0
                logit = jnp.where(ok, logit, NEG)
                top = jnp.max(logit, axis=1, keepdims=True)
                w = jnp.where(ok, jnp.exp(logit - top), 0.0)
                den = jnp.sum(w, axis=1, keepdims=True)
                mom = jnp.sum(w * tang, axis=1, keepdims=True)
                weights[rows, :] = w
                tangent[rows, :] = tang
                parts.append(jnp.where(lane == 0, top, jnp.where(lane == 1, den, jnp.where(lane == 2, mom, 0.0))))
            first = jnp.concatenate(parts[:4], axis=0)
            second = jnp.concatenate(parts[4:] + [jnp.zeros((64, 128), F32)], axis=0)
            stats[0:4, :] = jnp.transpose(first)[0:4, :]
            stats[4:8, :] = jnp.transpose(second)[0:4, :]


def row_block(j, q):
    return pl.BlockSpec((128, COLS), lambda i, tab: (q * 16 + tab[2 * i + j], 0))


def whole(shape):
    return pl.BlockSpec(shape, lambda i, tab: (0,) * len(shape))


def chunk_block(d, rows):
    return pl.BlockSpec((2, 2, rows, 128), lambda i, tab: (jnp.clip(i - 2 * d, 0, 1), 0, 0, 0))


def scores(tab, chunks, head, tangent_head, got=None, allowed=None):
    own = got is not None
    blocks = [row_block(j, q) for j in range(2) for q in range(2)]
    in_specs = [chunk_block(d, 2 * TOK) for d in range(4)] + blocks + blocks
    operands = list(chunks) + [head] * 4 + [tangent_head] * 4
    scratch = [pltpu.VMEM((2 * TOK, 512), BF16)]
    if own:
        in_specs += [whole((2 * TOK, COLS)), whole((TOK, 8))]
        operands += [got, allowed]
        shapes = [(TOK, COLS), (TOK, COLS), (8, 128)]
        scratch = [pltpu.VMEM((2 * TOK, COLS), F32)] + scratch
    else:
        shapes = [(2 * TOK, COLS)]
    out = pl.pallas_call(
        functools.partial(score_kernel, own=own),
        grid_spec=pltpu.PrefetchScalarGridSpec(
            num_scalar_prefetch=1,
            grid=(8,),
            in_specs=in_specs,
            out_specs=[whole(s) for s in shapes],
            scratch_shapes=scratch,
        ),
        out_shape=[jax.ShapeDtypeStruct(s, F32) for s in shapes],
        compiler_params=pltpu.CompilerParams(vmem_limit_bytes=VMEM, dimension_semantics=("arbitrary",)),
        cost_estimate=pl.CostEstimate(flops=6 * TOK * 4096 * COLS, bytes_accessed=20 << 20, transcendentals=0),
        name="scores_own" if own else "scores_other",
    )(tab, *operands)
    return out if own else out[0]


def product_kernel(every, mine, weights, tangent, out):
    cols = []
    for g in range(2):
        top = every[:, 4 * g, :]
        best = jnp.max(top, axis=0, keepdims=True)
        scale = jnp.exp(top - best)
        den = jnp.sum(every[:, 4 * g + 1, :] * scale, axis=0, keepdims=True)
        mom = jnp.sum(every[:, 4 * g + 2, :] * scale, axis=0, keepdims=True)
        if g:
            real = lax.broadcasted_iota(jnp.int32, (1, 128), 1) < 64
            den = jnp.where(real, den, 1.0)
        factor = jnp.exp(mine[4 * g : 4 * g + 1, :] - best) / den
        mean = mom / den
        row = lax.broadcasted_iota(jnp.int32, (128, 128), 0)
        cols.append(jnp.transpose(jnp.where(row == 0, factor, jnp.where(row == 1, mean, 0.0))))
    both = jnp.concatenate([cols[0], cols[1][:64]], axis=0)
    for r in range(0, TOK, 32):
        rows = slice(r, r + 32)
        p = (weights[rows, :] * both[rows, 0:1]) * (tangent[rows, :] - both[rows, 1:2])
        out[rows, :] = p.astype(BF16)


def make_product(every, mine, weights, tangent):
    return pl.pallas_call(
        product_kernel,
        out_shape=jax.ShapeDtypeStruct((TOK, COLS), BF16),
        compiler_params=pltpu.CompilerParams(vmem_limit_bytes=VMEM),
        name="product",
    )(every, mine, weights, tangent)


def back_kernel(tab, product, *refs):
    heads, outs = refs[:4], refs[4:]
    i = pl.program_id(0)
    right = jnp.concatenate([h[...] for h in heads], axis=0)
    term = lax.dot_general(product[...], right, (((1,), (1,)), ((), ())), preferred_element_type=F32).astype(BF16)
    for d in range(4):

        @pl.when(i // 2 == d)
        def _():
            for j in range(2):
                for q in range(2):
                    at = 128 * (2 * j + q)
                    outs[d][j, q] = term[:, at : at + 128]


def back(tab, product, head):
    blocks = [row_block(j, q) for j in range(2) for q in range(2)]
    return pl.pallas_call(
        back_kernel,
        grid_spec=pltpu.PrefetchScalarGridSpec(
            num_scalar_prefetch=1,
            grid=(8,),
            in_specs=[whole((TOK, COLS))] + blocks,
            out_specs=[chunk_block(d, TOK) for d in range(4)],
        ),
        out_shape=[jax.ShapeDtypeStruct((4, 2, TOK, 128), BF16)] * 4,
        compiler_params=pltpu.CompilerParams(vmem_limit_bytes=VMEM, dimension_semantics=("arbitrary",)),
        cost_estimate=pl.CostEstimate(flops=2 * TOK * 4096 * COLS, bytes_accessed=10 << 20, transcendentals=0),
        name="hidden_back",
    )(tab, product, *([head] * 4))


def outer_kernel(tabs, *refs):
    mine, others, p_own, p_other, out, held = refs[:4], refs[4:8], refs[8], refs[9], refs[10], refs[11]
    i = pl.program_id(0)

    @pl.when(i == 0)
    def _():
        for d in range(4):
            for m in range(4):
                for q in range(2):
                    held[q * 16 + tabs[4 * d + m], 0:TOK, :] = mine[d][m, q]
                    held[q * 16 + tabs[16 + 4 * d + m], TOK : 2 * TOK, :] = others[d][m, q]

    left = jnp.concatenate([held[4 * i + s] for s in range(4)], axis=1)
    right = jnp.concatenate([p_own[...], p_other[...]], axis=0)
    out[...] = lax.dot_general(left, right, (((0,), (0,)), ((), ())), preferred_element_type=F32).astype(BF16)


def outer(tabs, mine, others, p_own, p_other):
    rows = pl.BlockSpec((4, 2, TOK, 128), lambda i, tab: (0, 0, 0, 0))
    return pl.pallas_call(
        outer_kernel,
        grid_spec=pltpu.PrefetchScalarGridSpec(
            num_scalar_prefetch=1,
            grid=(8,),
            in_specs=[rows] * 8 + [whole((TOK, COLS))] * 2,
            out_specs=pl.BlockSpec((512, COLS), lambda i, tab: (i, 0)),
            scratch_shapes=[pltpu.VMEM((32, 2 * TOK, 128), BF16)],
        ),
        out_shape=jax.ShapeDtypeStruct((4096, COLS), BF16),
        compiler_params=pltpu.CompilerParams(vmem_limit_bytes=VMEM, dimension_semantics=("arbitrary",)),
        cost_estimate=pl.CostEstimate(flops=4 * TOK * 4096 * COLS, bytes_accessed=12 << 20, transcendentals=0),
        name="head_outer",
    )(tabs, *mine, *others, p_own, p_other)


def total(parts):
    out = parts[0].astype(F32)
    for p in parts[1:]:
        out = out + p.astype(F32)
    return out.astype(BF16)


def shards(hidden, tangent_hidden, head, tangent_head, allowed):
    k, v = lax.axis_index("dp"), lax.axis_index("vocab")
    y, x = (v // 4) % 4, v % 4
    step = jnp.arange(16, dtype=jnp.int32)
    d, m = step // 4, step % 4
    by_x, by_y = m * 4 + (x - d + 4) % 4, ((y - d + 4) % 4) * 4 + m
    tab_own, tab_other = jnp.where(k == 0, by_x, by_y), jnp.where(k == 0, by_y, by_x)

    rows = jnp.concatenate([hidden, tangent_hidden], axis=0)
    column = spread(rows, depth_groups())
    plane = spread(column, middle_groups())
    mine = plane[:, :2]
    other = permute(plane[:, 2:], swap_pairs())
    others = [other] + [permute(other, shift(False, s)) for s in (1, 2, 3)]
    owns = [mine] + [permute(mine, shift(True, s)) for s in (1, 2, 3)]

    sent = scores(tab_other, others, head, tangent_head)
    got = permute(sent, swap_pairs())
    weights, tangent, stats = scores(tab_own, owns, head, tangent_head, got, allowed)
    every = lax.all_to_all(
        jnp.broadcast_to(stats[None], (64, 8, 128)), "vocab", split_axis=0, concat_axis=0, tiled=True
    )
    p_own = make_product(every, stats, weights, tangent)
    p_other = permute(p_own, swap_pairs())

    terms = back(tab_own, p_own, head)
    sums = total([terms[0]] + [permute(terms[s], shift(True, -s)) for s in (1, 2, 3)])
    terms = back(tab_other, p_other, head)
    sums_other = total([terms[0]] + [permute(terms[s], shift(False, -s)) for s in (1, 2, 3)])
    head_product = outer(jnp.concatenate([tab_own, tab_other]), owns, others, p_own, p_other)
    rest = permute(sums_other, swap_pairs())
    slab = jnp.concatenate([sums, rest], axis=1).reshape(16, TOK, 128)
    arrived = exchange(slab, plane_groups())
    hidden_product = jnp.sum(arrived.astype(F32), axis=0).astype(BF16)
    return head_product, hidden_product


def solution(mesh):
    place = P("dp", "vocab")
    return jax.shard_map(shards, mesh=mesh, in_specs=(place,) * 5, out_specs=(place, place), check_vma=False)
```

```python
import functools

import jax
import jax.numpy as jnp
from jax import lax
from jax.experimental import pallas as pl
from jax.experimental.pallas import tpu as pltpu
from jax.sharding import PartitionSpec as P

AXES = ("dp", "vocab")
SIDE = 4
TOK = 192
COLS = 1024
NEG = -1e30
WHOLE = pl.BlockSpec(memory_space=pltpu.VMEM)
SCALARS = pl.BlockSpec(memory_space=pltpu.SMEM)
ORDER = [(s, q) for s in range(4) for q in range(2)]
F32 = jnp.float32
BF16 = jnp.bfloat16


def flat(k, z, y, x):
    return k * 64 + (z % 4) * 16 + (y % 4) * 4 + x % 4


def sites():
    return [(k, z, y, x) for k in range(2) for z in range(4) for y in range(4) for x in range(4)]


def last_shift(d):
    return [(flat(k, z, y, x), flat(k, z, y, x + d) if k == 0 else flat(k, z, y + d, x)) for k, z, y, x in sites()]


def mid_shift(d):
    return [(flat(k, z, y, x), flat(k, z, y + d, x) if k == 0 else flat(k, z, y, x + d)) for k, z, y, x in sites()]


def swap_pairs():
    return [(flat(k, z, y, x), flat(1 - k, z, y, x)) for k, z, y, x in sites()]


def depth_pairs(c):
    pairs = []
    for k, z, y, x in sites():
        e = (z + c) % 4
        pairs.append((flat(k, z, y, x), flat(e // 2, 2 * k + e % 2, y, x)))
    return pairs


def depth_groups():
    return [[flat(k, r + 2 * k, y, x) for r in range(4)] for k in range(2) for y in range(4) for x in range(4)]


def permute(value, pairs):
    return lax.ppermute(value, AXES, pairs)


def spread(value, groups):
    full = jnp.broadcast_to(value[None], (len(groups[0]),) + value.shape)
    return lax.all_to_all(full, AXES, split_axis=0, concat_axis=0, tiled=True, axis_index_groups=groups)


def params(mib):
    return pltpu.CompilerParams(vmem_limit_bytes=mib << 20)


def cost(flops, moved):
    return pl.CostEstimate(flops=flops, bytes_accessed=moved, transcendentals=0)


def load_kernel(a, b, a_out, b_out, sems):
    copies = [pltpu.make_async_copy(a, a_out, sems.at[0]), pltpu.make_async_copy(b, b_out, sems.at[1])]
    for c in copies:
        c.start()
    for c in copies:
        c.wait()


def load_near(a, b):
    return pl.pallas_call(
        load_kernel,
        in_specs=[pl.BlockSpec(memory_space=pl.ANY)] * 2,
        out_specs=[WHOLE] * 2,
        out_shape=[pltpu.VMEM(a.shape, a.dtype), pltpu.VMEM(b.shape, b.dtype)],
        scratch_shapes=[pltpu.SemaphoreType.DMA((2,))],
        compiler_params=params(4),
        cost_estimate=cost(0, 48 << 20),
        name="load_near",
    )(a, b)


def rows_at(place, d, s, q):
    last, mid = lax.rem(place[1] + 4 - d, 4), lax.rem(place[2] + 4 - s, 4)
    r = jnp.where(place[0] == 0, 4 * mid + last, 4 * last + mid)
    return pl.ds(pl.multiple_of((16 * q + r) * 128, 128), 128)


def score_kernel(place, *refs, steps, final):
    n = len(steps)
    chunks, (head, thead), refs = refs[:n], refs[n : n + 2], refs[n + 2 :]
    if final:
        early, got, allowed, weights, tangent, stats, acc = refs
    else:
        (acc,) = refs
    spots = [rows_at(place, d, s, q) for d in steps for s, q in ORDER]
    left = jnp.concatenate([c[s, q] for c in chunks for s, q in ORDER], axis=1)
    for n in range(4):
        cols = slice(256 * n, 256 * n + 256)
        right = jnp.concatenate([head[r, cols] for r in spots], axis=0)
        turn = jnp.concatenate([thead[r, cols] for r in spots], axis=0)
        both = jnp.dot(left, right, preferred_element_type=F32)
        more = jnp.dot(left[:TOK], turn, preferred_element_type=F32)
        acc[:TOK, cols] = both[:TOK]
        acc[TOK:, cols] = both[TOK:] + more
    if not final:
        return
    lane = lax.broadcasted_iota(jnp.int32, (32, 128), 1)
    parts = []
    for r in range(0, TOK, 32):
        rows, trows = slice(r, r + 32), slice(TOK + r, TOK + r + 32)
        logit = acc[rows, :] + early[rows, :] + got[rows, :]
        tang = acc[trows, :] + early[trows, :] + got[trows, :]
        ok = jnp.concatenate([jnp.broadcast_to(allowed[rows, b : b + 1], (32, 128)) for b in range(8)], axis=1) > 0
        logit = jnp.where(ok, logit, NEG)
        top = jnp.max(logit, axis=1, keepdims=True)
        w = jnp.where(ok, jnp.exp(logit - top), 0.0)
        den = jnp.sum(w, axis=1, keepdims=True)
        mom = jnp.sum(w * tang, axis=1, keepdims=True)
        weights[rows, :] = w
        tangent[rows, :] = tang
        parts.append(jnp.where(lane == 0, top, jnp.where(lane == 1, den, jnp.where(lane == 2, mom, 0.0))))
    first = jnp.concatenate(parts[:4], axis=0)
    second = jnp.concatenate(parts[4:] + [jnp.zeros((64, 128), F32)], axis=0)
    stats[0:4, :] = jnp.transpose(first)[0:4, :]
    stats[4:8, :] = jnp.transpose(second)[0:4, :]


def scores(place, steps, chunks, head, thead, name, late=()):
    final = len(late) > 0
    operands = [place, *chunks, head, thead, *late]
    shapes = [(TOK, COLS), (TOK, COLS), (8, 128)] if final else [(2 * TOK, COLS)]
    out = pl.pallas_call(
        functools.partial(score_kernel, steps=steps, final=final),
        in_specs=[SCALARS] + [WHOLE] * (len(operands) - 1),
        out_specs=[WHOLE] * len(shapes),
        out_shape=[jax.ShapeDtypeStruct(s, F32) for s in shapes],
        scratch_shapes=[pltpu.VMEM((2 * TOK, COLS), F32)] if final else [],
        compiler_params=params(28),
        cost_estimate=cost(60 * TOK * 1024 * len(steps) * COLS, 5 * len(steps) << 20),
        name=name,
    )(*operands)
    return out if final else out[0]


def product_kernel(every, mine, weights, tangent, out):
    cols = []
    for g in range(2):
        top = every[:, 4 * g, :]
        best = jnp.max(top, axis=0, keepdims=True)
        scale = jnp.exp(top - best)
        den = jnp.sum(every[:, 4 * g + 1, :] * scale, axis=0, keepdims=True)
        mom = jnp.sum(every[:, 4 * g + 2, :] * scale, axis=0, keepdims=True)
        if g:
            real = lax.broadcasted_iota(jnp.int32, (1, 128), 1) < 64
            den = jnp.where(real, den, 1.0)
        factor = jnp.exp(mine[4 * g : 4 * g + 1, :] - best) / den
        mean = mom / den
        row = lax.broadcasted_iota(jnp.int32, (128, 128), 0)
        cols.append(jnp.transpose(jnp.where(row == 0, factor, jnp.where(row == 1, mean, 0.0))))
    both = jnp.concatenate([cols[0], cols[1][:64]], axis=0)
    for r in range(0, TOK, 32):
        rows = slice(r, r + 32)
        p = (weights[rows, :] * both[rows, 0:1]) * (tangent[rows, :] - both[rows, 1:2])
        out[rows, :] = p.astype(BF16)


def make_product(every, mine, weights, tangent):
    return pl.pallas_call(
        product_kernel,
        in_specs=[WHOLE] * 4,
        out_specs=WHOLE,
        out_shape=jax.ShapeDtypeStruct((TOK, COLS), BF16),
        compiler_params=params(16),
        name="product",
    )(every, mine, weights, tangent)


def back_kernel(place, product, head, *refs):
    outs, turned = refs[:4], refs[4]
    turned[...] = jnp.transpose(product[...].astype(F32)).astype(BF16)
    for d in (1, 3, 2, 0):
        rows = jnp.concatenate([head[rows_at(place, d, s, q), :] for s, q in ORDER], axis=0)
        term = jnp.dot(rows, turned[...], preferred_element_type=F32).astype(BF16)
        for s in range(4):
            low, high = term[256 * s : 256 * s + 128], term[256 * s + 128 : 256 * s + 256]
            outs[d][s, 0] = low[:, :128]
            outs[d][s, 1] = high[:, :128]
            outs[d][s, 2] = jnp.concatenate([low[:, 128:], high[:, 128:]], axis=1)


def back(place, product, head, name):
    return pl.pallas_call(
        back_kernel,
        in_specs=[SCALARS, WHOLE, WHOLE],
        out_specs=[WHOLE] * 4,
        out_shape=[jax.ShapeDtypeStruct((4, 3, 128, 128), BF16)] * 4,
        scratch_shapes=[pltpu.VMEM((COLS, TOK), BF16)],
        compiler_params=params(20),
        cost_estimate=cost(2 * TOK * 4096 * COLS, 10 << 20),
        name=name,
    )(place, product, head)


def line_sum_kernel(*refs):
    own, other, outs = refs[:4], refs[4:8], refs[8:]
    for s in range(4):
        for t, terms in enumerate((own, other)):
            for b in range(3):
                value = terms[0][s, b].astype(F32)
                for term in terms[1:]:
                    value = value + term[s, b].astype(F32)
                outs[s][t, b] = value.astype(BF16)


def line_sum(own, other):
    return pl.pallas_call(
        line_sum_kernel,
        in_specs=[WHOLE] * 8,
        out_specs=[WHOLE] * 4,
        out_shape=[jax.ShapeDtypeStruct((2, 3, 128, 128), BF16)] * 4,
        compiler_params=params(16),
        name="line_sum",
    )(*own, *other)


def plane_sum_kernel(place, *refs):
    terms, outs, held = refs[:4], refs[4:8], refs[8]
    for t in range(2):
        turned = []
        for b in range(3):
            value = terms[0][t, b].astype(F32)
            for term in terms[1:]:
                value = value + term[t, b].astype(F32)
            turned.append(jnp.transpose(value).astype(BF16))
        for q in range(2):
            held[2 * t + q, 0:128] = turned[q]
            held[2 * t + q, 128:TOK] = turned[2][64 * q : 64 * q + 64]
    for c in range(4):
        e = lax.rem(place[3] + c, 4)
        t = jnp.where(e // 2 == place[0], 0, 1)
        outs[c][...] = held[2 * t + lax.rem(e, 2)]


def plane_sum(place, terms):
    return pl.pallas_call(
        plane_sum_kernel,
        in_specs=[SCALARS] + [WHOLE] * 4,
        out_specs=[WHOLE] * 4,
        out_shape=[jax.ShapeDtypeStruct((TOK, 128), BF16)] * 4,
        scratch_shapes=[pltpu.VMEM((4, TOK, 128), BF16)],
        compiler_params=params(16),
        name="plane_sum",
    )(place, *terms)


def outer_kernel(place, *refs):
    mine, others, p_own, p_other, out, held = refs[:4], refs[4:8], refs[8], refs[9], refs[10], refs[11]
    i = pl.program_id(0)

    @pl.when(i == 0)
    def _():
        for d in range(4):
            for s, q in ORDER:
                rows = rows_at(place, d, s, q)
                held[rows.start // 128, 0:TOK] = mine[d][s, q]
                held[rows.start // 128, TOK : 2 * TOK] = others[d][s, q]

    left = jnp.concatenate([held[4 * i + j] for j in range(4)], axis=1)
    right = jnp.concatenate([p_own[...], p_other[...]], axis=0)
    out[...] = lax.dot_general(left, right, (((0,), (0,)), ((), ())), preferred_element_type=F32).astype(BF16)


def outer(place, mine, others, p_own, p_other):
    rows = pl.BlockSpec((4, 2, TOK, 128), lambda i: (0, 0, 0, 0))
    whole = pl.BlockSpec((TOK, COLS), lambda i: (0, 0))
    return pl.pallas_call(
        outer_kernel,
        grid=(8,),
        in_specs=[SCALARS] + [rows] * 8 + [whole] * 2,
        out_specs=pl.BlockSpec((512, COLS), lambda i: (i, 0)),
        out_shape=jax.ShapeDtypeStruct((4096, COLS), BF16),
        scratch_shapes=[pltpu.VMEM((32, 2 * TOK, 128), BF16)],
        compiler_params=params(24),
        cost_estimate=cost(4 * TOK * 4096 * COLS, 12 << 20),
        name="head_outer",
    )(place, *mine, *others, p_own, p_other)


def shards(hidden, tangent_hidden, head, tangent_head, allowed):
    k, v = lax.axis_index("dp"), lax.axis_index("vocab")
    z, y, x = v // 16, (v // 4) % 4, v % 4
    place = jnp.stack([k, jnp.where(k == 0, x, y), jnp.where(k == 0, y, x), z]).astype(jnp.int32)
    head_near, thead_near = load_near(*(pltpu.with_memory_space_constraint(h, pltpu.HBM) for h in (head, tangent_head)))

    column = spread(jnp.concatenate([hidden, tangent_hidden], axis=0), depth_groups())
    both = jnp.stack([column[:2], permute(column[2:], swap_pairs())])
    middle = [both] + [permute(both, mid_shift(s)) for s in (1, 2, 3)]
    own = jnp.stack([m[0] for m in middle])
    other = jnp.stack([m[1] for m in middle])
    other1, other3 = permute(other, last_shift(1)), permute(other, last_shift(-1))
    own, other1, other3 = lax.optimization_barrier((own, other1, other3))
    other2 = permute(other1, last_shift(1))
    own3, own1 = permute(own, last_shift(-1)), permute(own, last_shift(1))
    own2 = permute(own3, last_shift(-1))
    owns, others = [own, own1, own2, own3], [other, other1, other2, other3]

    sent = scores(place, (0, 1, 3, 2), [other, other1, other3, other2], head_near, thead_near, "scores_other")
    got = permute(sent, swap_pairs())
    early = scores(place, (0, 1, 3), [own, own1, own3], head_near, thead_near, "scores_early")
    weights, tangent, stats = scores(
        place, (2,), [own2], head_near, thead_near, "scores_final", (early, got, allowed)
    )
    every = lax.all_to_all(
        jnp.broadcast_to(stats[None], (64, 8, 128)), "vocab", split_axis=0, concat_axis=0, tiled=True
    )
    p_own = make_product(every, stats, weights, tangent)
    p_other = permute(p_own, swap_pairs())

    terms = back(place, p_own, head_near, "back_own")
    mine = [terms[0]] + [permute(terms[d], last_shift(-d)) for d in (1, 3, 2)]
    terms = back(place, p_other, head_near, "back_other")
    theirs = [terms[0]] + [permute(terms[d], last_shift(-d)) for d in (1, 3, 2)]
    head_product = outer(place, owns, others, p_own, p_other)
    head_product, theirs[0] = lax.optimization_barrier((head_product, theirs[0]))
    lines = line_sum(mine, theirs)
    planes = plane_sum(place, [lines[0]] + [permute(lines[s], mid_shift(-s)) for s in (1, 2, 3)])
    ends = [permute(p, depth_pairs(c)) for c, p in enumerate(planes)]
    hidden_product = sum(e.astype(F32) for e in ends).astype(BF16)
    return head_product, hidden_product


def solution(mesh):
    place = P("dp", "vocab")
    return jax.shard_map(shards, mesh=mesh, in_specs=(place,) * 5, out_specs=(place, place), check_vma=False)
```

```python
import functools

import jax
import jax.numpy as jnp
from jax import lax
from jax.experimental import pallas as pl
from jax.experimental.pallas import tpu as pltpu
from jax.sharding import PartitionSpec as P

AXES = ("dp", "vocab")
SIDE = 4
TOK = 192
COLS = 1024
NEG = -1e30
WHOLE = pl.BlockSpec(memory_space=pltpu.VMEM)
SCALARS = pl.BlockSpec(memory_space=pltpu.SMEM)
ORDER = [(s, q) for s in range(4) for q in range(2)]
F32 = jnp.float32
BF16 = jnp.bfloat16


def flat(k, z, y, x):
    return k * 64 + (z % 4) * 16 + (y % 4) * 4 + x % 4


def sites():
    return [(k, z, y, x) for k in range(2) for z in range(4) for y in range(4) for x in range(4)]


def last_shift(d):
    return [(flat(k, z, y, x), flat(k, z, y, x + d) if k == 0 else flat(k, z, y + d, x)) for k, z, y, x in sites()]


def mid_shift(d):
    return [(flat(k, z, y, x), flat(k, z, y + d, x) if k == 0 else flat(k, z, y, x + d)) for k, z, y, x in sites()]


def swap_pairs():
    return [(flat(k, z, y, x), flat(1 - k, z, y, x)) for k, z, y, x in sites()]


def start_pairs(c):
    return [(flat(k, z, y, x), flat(z // 2, 2 * k + z % 2 + c, y, x)) for k, z, y, x in sites()]


def end_pairs():
    return [(flat(k, z, y, x), flat(z // 2, 2 * k + z % 2, y, x)) for k, z, y, x in sites()]


def plane_groups():
    return [[flat(0, r, m, x) for m in range(4) for r in range(4)] for x in range(4)] + [
        [flat(1, r, y, m) for m in range(4) for r in range(4)] for y in range(4)
    ]


def permute(value, pairs):
    return lax.ppermute(value, AXES, pairs)


def params(mib):
    return pltpu.CompilerParams(vmem_limit_bytes=mib << 20)


def cost(flops, moved):
    return pl.CostEstimate(flops=flops, bytes_accessed=moved, transcendentals=0)


def load_kernel(a, b, a_out, b_out, sems):
    copies = [pltpu.make_async_copy(a, a_out, sems.at[0]), pltpu.make_async_copy(b, b_out, sems.at[1])]
    for c in copies:
        c.start()
    for c in copies:
        c.wait()


def load_near(a, b):
    return pl.pallas_call(
        load_kernel,
        in_specs=[pl.BlockSpec(memory_space=pl.ANY)] * 2,
        out_specs=[WHOLE] * 2,
        out_shape=[pltpu.VMEM(a.shape, a.dtype), pltpu.VMEM(b.shape, b.dtype)],
        scratch_shapes=[pltpu.SemaphoreType.DMA((2,))],
        compiler_params=params(4),
        cost_estimate=cost(0, 48 << 20),
        name="load_near",
    )(a, b)


def join_kernel(a, b, out, sems):
    copies = [
        pltpu.make_async_copy(a, out.at[0:TOK], sems.at[0]),
        pltpu.make_async_copy(b, out.at[TOK : 2 * TOK], sems.at[1]),
    ]
    for c in copies:
        c.start()
    for c in copies:
        c.wait()


def join(a, b):
    return pl.pallas_call(
        join_kernel,
        in_specs=[pl.BlockSpec(memory_space=pl.ANY)] * 2,
        out_specs=WHOLE,
        out_shape=jax.ShapeDtypeStruct((2 * TOK, 128), BF16),
        scratch_shapes=[pltpu.SemaphoreType.DMA((2,))],
        compiler_params=params(2),
        name="join",
    )(a, b)


def arrange_kernel(place, *refs):
    blocks, out = refs[:4], refs[4]
    for c in range(4):
        e = lax.rem(place[3] + 4 - c, 4)
        out[jnp.where(e // 2 == place[0], 0, 1), lax.rem(e, 2)] = blocks[c][...]


def arrange(place, blocks):
    return pl.pallas_call(
        arrange_kernel,
        in_specs=[SCALARS] + [WHOLE] * 4,
        out_specs=WHOLE,
        out_shape=jax.ShapeDtypeStruct((2, 2, 2 * TOK, 128), BF16),
        compiler_params=params(8),
        name="arrange",
    )(place, *blocks)


def rows_at(place, d, s, q):
    last, mid = lax.rem(place[1] + 4 - d, 4), lax.rem(place[2] + 4 - s, 4)
    r = jnp.where(place[0] == 0, 4 * mid + last, 4 * last + mid)
    return pl.ds(pl.multiple_of((16 * q + r) * 128, 128), 128)


def score_kernel(place, *refs, steps, added, final):
    n = len(steps)
    chunks, (head, thead), refs = refs[:n], refs[n : n + 2], refs[n + 2 :]
    early, refs = (refs[0], refs[1:]) if added else (None, refs)
    if final:
        got, allowed, weights, tangent, stats, acc = refs
    else:
        (acc,) = refs
    spots = [rows_at(place, d, s, q) for d in steps for s, q in ORDER]
    left = jnp.concatenate([c[s, q] for c in chunks for s, q in ORDER], axis=1)
    for n in range(4):
        cols = slice(256 * n, 256 * n + 256)
        right = jnp.concatenate([head[r, cols] for r in spots], axis=0)
        turn = jnp.concatenate([thead[r, cols] for r in spots], axis=0)
        both = jnp.dot(left, right, preferred_element_type=F32)
        more = jnp.dot(left[:TOK], turn, preferred_element_type=F32)
        if added:
            both = both + early[:, cols]
        acc[:TOK, cols] = both[:TOK]
        acc[TOK:, cols] = both[TOK:] + more
    if not final:
        return
    lane = lax.broadcasted_iota(jnp.int32, (32, 128), 1)
    parts = []
    for r in range(0, TOK, 32):
        rows, trows = slice(r, r + 32), slice(TOK + r, TOK + r + 32)
        logit = acc[rows, :] + got[rows, :]
        tang = acc[trows, :] + got[trows, :]
        ok = jnp.concatenate([jnp.broadcast_to(allowed[rows, b : b + 1], (32, 128)) for b in range(8)], axis=1) > 0
        logit = jnp.where(ok, logit, NEG)
        top = jnp.max(logit, axis=1, keepdims=True)
        w = jnp.where(ok, jnp.exp(logit - top), 0.0)
        den = jnp.sum(w, axis=1, keepdims=True)
        mom = jnp.sum(w * tang, axis=1, keepdims=True)
        weights[rows, :] = w
        tangent[rows, :] = tang
        parts.append(jnp.where(lane == 0, top, jnp.where(lane == 1, den, jnp.where(lane == 2, mom, 0.0))))
    first = jnp.concatenate(parts[:4], axis=0)
    second = jnp.concatenate(parts[4:] + [jnp.zeros((64, 128), F32)], axis=0)
    stats[0:4, :] = jnp.transpose(first)[0:4, :]
    stats[4:8, :] = jnp.transpose(second)[0:4, :]


def scores(place, steps, chunks, head, thead, name, weight, early=None, late=()):
    added, final = early is not None, len(late) > 0
    operands = [place, *chunks, head, thead, *([early] if added else []), *late]
    shapes = [(TOK, COLS), (TOK, COLS), (8, 128)] if final else [(2 * TOK, COLS)]
    out = pl.pallas_call(
        functools.partial(score_kernel, steps=steps, added=added, final=final),
        in_specs=[SCALARS] + [WHOLE] * (len(operands) - 1),
        out_specs=[WHOLE] * len(shapes),
        out_shape=[jax.ShapeDtypeStruct(s, F32) for s in shapes],
        scratch_shapes=[pltpu.VMEM((2 * TOK, COLS), F32)] if final else [],
        compiler_params=params(12),
        cost_estimate=cost(weight * 6 * TOK * 4096 * COLS, weight << 20),
        name=name,
    )(*operands)
    return out if final else out[0]


def product_kernel(every, mine, weights, tangent, out):
    cols = []
    for g in range(2):
        top = every[:, 4 * g, :]
        best = jnp.max(top, axis=0, keepdims=True)
        scale = jnp.exp(top - best)
        den = jnp.sum(every[:, 4 * g + 1, :] * scale, axis=0, keepdims=True)
        mom = jnp.sum(every[:, 4 * g + 2, :] * scale, axis=0, keepdims=True)
        if g:
            real = lax.broadcasted_iota(jnp.int32, (1, 128), 1) < 64
            den = jnp.where(real, den, 1.0)
        factor = jnp.exp(mine[4 * g : 4 * g + 1, :] - best) / den
        mean = mom / den
        row = lax.broadcasted_iota(jnp.int32, (128, 128), 0)
        cols.append(jnp.transpose(jnp.where(row == 0, factor, jnp.where(row == 1, mean, 0.0))))
    both = jnp.concatenate([cols[0], cols[1][:64]], axis=0)
    for r in range(0, TOK, 32):
        rows = slice(r, r + 32)
        p = (weights[rows, :] * both[rows, 0:1]) * (tangent[rows, :] - both[rows, 1:2])
        out[rows, :] = p.astype(BF16)


def make_product(every, mine, weights, tangent):
    return pl.pallas_call(
        product_kernel,
        in_specs=[WHOLE] * 4,
        out_specs=WHOLE,
        out_shape=jax.ShapeDtypeStruct((TOK, COLS), BF16),
        compiler_params=params(16),
        name="product",
    )(every, mine, weights, tangent)


def back_kernel(place, product, head, *refs):
    outs, turned = refs[:4], refs[4]
    turned[...] = jnp.transpose(product[...].astype(F32)).astype(BF16)
    for d in (1, 3, 2, 0):
        rows = jnp.concatenate([head[rows_at(place, d, s, q), :] for s, q in ORDER], axis=0)
        term = jnp.dot(rows, turned[...], preferred_element_type=F32).astype(BF16)
        for s in range(4):
            low, high = term[256 * s : 256 * s + 128], term[256 * s + 128 : 256 * s + 256]
            outs[d][s, 0] = low[:, :128]
            outs[d][s, 1] = high[:, :128]
            outs[d][s, 2] = jnp.concatenate([low[:, 128:], high[:, 128:]], axis=1)


def back(place, product, head, name):
    return pl.pallas_call(
        back_kernel,
        in_specs=[SCALARS, WHOLE, WHOLE],
        out_specs=[WHOLE] * 4,
        out_shape=[jax.ShapeDtypeStruct((4, 3, 128, 128), BF16)] * 4,
        scratch_shapes=[pltpu.VMEM((COLS, TOK), BF16)],
        compiler_params=params(8),
        cost_estimate=cost(2 * TOK * 4096 * COLS, 10 << 20),
        name=name,
    )(place, product, head)


def line_sum_kernel(place, *refs):
    own, other, out = refs[:4], refs[4:8], refs[8]
    for s in range(4):
        mid = lax.rem(place[2] + 4 - s, 4)
        for t, terms in enumerate((own, other)):
            half = jnp.where(place[0] == t, 0, 1)
            sums = []
            for b in range(3):
                value = terms[0][s, b].astype(F32)
                for term in terms[1:]:
                    value = value + term[s, b].astype(F32)
                sums.append(value.astype(BF16))
            for q in range(2):
                tail = sums[2][:, 64 * q : 64 * q + 64]
                to = 4 * mid + 2 * half + q
                out[to, 0:128] = sums[q]
                out[to, 128:TOK] = jnp.concatenate([tail[:64], tail[64:]], axis=1)


def line_sum(place, own, other):
    return pl.pallas_call(
        line_sum_kernel,
        in_specs=[SCALARS] + [WHOLE] * 8,
        out_specs=WHOLE,
        out_shape=jax.ShapeDtypeStruct((16, TOK, 128), BF16),
        compiler_params=params(16),
        name="line_sum",
    )(place, *own, *other)


def plane_sum_kernel(terms, out):
    value = terms[0].astype(F32)
    for j in range(1, 16):
        value = value + terms[j].astype(F32)
    fold = value[128:]
    out[0:128] = jnp.transpose(value[:128]).astype(BF16)
    tail = jnp.concatenate([fold[:, :64], fold[:, 64:]], axis=0)
    out[128:TOK] = jnp.transpose(tail).astype(BF16)


def plane_sum(terms):
    return pl.pallas_call(
        plane_sum_kernel,
        in_specs=[WHOLE],
        out_specs=WHOLE,
        out_shape=jax.ShapeDtypeStruct((TOK, 128), BF16),
        compiler_params=params(8),
        name="plane_sum",
    )(terms)


def outer_kernel(place, *refs):
    mine, others, p_own, p_other, out, held = refs[:4], refs[4:8], refs[8], refs[9], refs[10], refs[11]
    i = pl.program_id(0)

    @pl.when(i == 0)
    def _():
        for d in range(4):
            for s, q in ORDER:
                rows = rows_at(place, d, s, q)
                held[rows.start // 128, 0:TOK] = mine[d][s, q]
                held[rows.start // 128, TOK : 2 * TOK] = others[d][s, q]

    left = jnp.concatenate([held[4 * i + j] for j in range(4)], axis=1)
    right = jnp.concatenate([p_own[...], p_other[...]], axis=0)
    out[...] = lax.dot_general(left, right, (((0,), (0,)), ((), ())), preferred_element_type=F32).astype(BF16)


def outer(place, mine, others, p_own, p_other):
    rows = pl.BlockSpec((4, 2, TOK, 128), lambda i: (0, 0, 0, 0))
    whole = pl.BlockSpec((TOK, COLS), lambda i: (0, 0))
    return pl.pallas_call(
        outer_kernel,
        grid=(8,),
        in_specs=[SCALARS] + [rows] * 8 + [whole] * 2,
        out_specs=pl.BlockSpec((512, COLS), lambda i: (i, 0)),
        out_shape=jax.ShapeDtypeStruct((4096, COLS), BF16),
        scratch_shapes=[pltpu.VMEM((32, 2 * TOK, 128), BF16)],
        compiler_params=params(16),
        cost_estimate=cost(4 * TOK * 4096 * COLS, 12 << 20),
        name="head_outer",
    )(place, *mine, *others, p_own, p_other)


def shards(hidden, tangent_hidden, head, tangent_head, allowed):
    k, v = lax.axis_index("dp"), lax.axis_index("vocab")
    z, y, x = v // 16, (v // 4) % 4, v % 4
    place = jnp.stack([k, jnp.where(k == 0, x, y), jnp.where(k == 0, y, x), z]).astype(jnp.int32)
    head_near, thead_near = load_near(*(pltpu.with_memory_space_constraint(h, pltpu.HBM) for h in (head, tangent_head)))

    rows = join(*(pltpu.with_memory_space_constraint(h, pltpu.HBM) for h in (hidden, tangent_hidden)))
    both = arrange(place, [permute(rows, start_pairs(c)) for c in range(4)])
    middle = [both] + [permute(both, mid_shift(s)) for s in (1, 2, 3)]
    own = jnp.stack([m[0] for m in middle])
    other = jnp.stack([m[1] for m in middle])
    other1, other3, own3 = permute(other, last_shift(1)), permute(other, last_shift(-1)), permute(own, last_shift(-1))
    other2 = permute(other1, last_shift(1))
    own, other3, own3, head_near, thead_near = lax.optimization_barrier((own, other3, own3, head_near, thead_near))
    own2, own1 = permute(own3, last_shift(-1)), permute(own, last_shift(1))
    owns, others = [own, own1, own2, own3], [other, other1, other2, other3]

    near = (head_near, thead_near)
    sent = scores(place, (0, 1, 3, 2), [other, other1, other3, other2], *near, "scores_other", 10)
    got = permute(sent, swap_pairs())
    early = scores(place, (0, 3), [own, own3], *near, "own_first", 10)
    early = scores(place, (2,), [own2], *near, "own_next", 0, early)
    weights, tangent, stats = scores(place, (1,), [own1], *near, "own_last", 0, early, (got, allowed))
    every = lax.all_to_all(
        jnp.broadcast_to(stats[None], (64, 8, 128)), "vocab", split_axis=0, concat_axis=0, tiled=True
    )
    p_own = make_product(every, stats, weights, tangent)
    p_other = permute(p_own, swap_pairs())

    terms = back(place, p_own, head_near, "back_own")
    mine = [terms[0]] + [permute(terms[d], last_shift(-d)) for d in (1, 3, 2)]
    terms = back(place, p_other, head_near, "back_other")
    theirs = [terms[0]] + [permute(terms[d], last_shift(-d)) for d in (1, 3, 2)]
    head_product = outer(place, owns, others, p_own, p_other)
    head_product, theirs[0] = lax.optimization_barrier((head_product, theirs[0]))
    lines = line_sum(place, mine, theirs)
    arrived = lax.all_to_all(lines, AXES, split_axis=0, concat_axis=0, tiled=True, axis_index_groups=plane_groups())
    hidden_product = permute(plane_sum(arrived), end_pairs())
    return head_product, hidden_product


def solution(mesh):
    place = P("dp", "vocab")
    return jax.shard_map(shards, mesh=mesh, in_specs=(place,) * 5, out_specs=(place, place), check_vma=False)
```

```python
import functools

import jax
import jax.numpy as jnp
from jax import lax
from jax.experimental import pallas as pl
from jax.experimental.pallas import tpu as pltpu
from jax.sharding import PartitionSpec as P

AXES = ("dp", "vocab")
SIDE = 4
TOK = 192
COLS = 1024
NEG = -1e30
WHOLE = pl.BlockSpec(memory_space=pltpu.VMEM)
SCALARS = pl.BlockSpec(memory_space=pltpu.SMEM)
ORDER = [(s, q) for s in range(4) for q in range(2)]
F32 = jnp.float32
BF16 = jnp.bfloat16


def flat(k, z, y, x):
    return k * 64 + (z % 4) * 16 + (y % 4) * 4 + x % 4


def sites():
    return [(k, z, y, x) for k in range(2) for z in range(4) for y in range(4) for x in range(4)]


def last_shift(d):
    return [(flat(k, z, y, x), flat(k, z, y, x + d) if k == 1 else flat(k, z, y + d, x)) for k, z, y, x in sites()]


def mid_shift(d):
    return [(flat(k, z, y, x), flat(k, z, y + d, x) if k == 1 else flat(k, z, y, x + d)) for k, z, y, x in sites()]


def swap_pairs():
    return [(flat(k, z, y, x), flat(1 - k, z, y, x)) for k, z, y, x in sites()]


def start_pairs(c):
    return [(flat(k, z, y, x), flat(z // 2, 2 * k + z % 2 + c, y, x)) for k, z, y, x in sites()]


def plane_groups():
    return [[flat(1, r, m, x) for m in range(4) for r in range(4)] for x in range(4)] + [
        [flat(0, r, y, m) for m in range(4) for r in range(4)] for y in range(4)
    ]


def permute(value, pairs):
    return lax.ppermute(value, AXES, pairs)


def params(mib):
    return pltpu.CompilerParams(vmem_limit_bytes=mib << 20)


def cost(flops, moved):
    return pl.CostEstimate(flops=flops, bytes_accessed=moved, transcendentals=0)


def load_kernel(a, out, sem):
    copy = pltpu.make_async_copy(a, out, sem)
    copy.start()
    copy.wait()


def load_near(a, name):
    return pl.pallas_call(
        load_kernel,
        in_specs=[pl.BlockSpec(memory_space=pl.ANY)],
        out_specs=WHOLE,
        out_shape=pltpu.VMEM(a.shape, a.dtype),
        scratch_shapes=[pltpu.SemaphoreType.DMA],
        compiler_params=params(2),
        cost_estimate=cost(0, 24 << 20),
        name=name,
    )(pltpu.with_memory_space_constraint(a, pltpu.HBM))


def join_kernel(a, b, out, sems):
    copies = [
        pltpu.make_async_copy(a, out.at[0:TOK], sems.at[0]),
        pltpu.make_async_copy(b, out.at[TOK : 2 * TOK], sems.at[1]),
    ]
    for c in copies:
        c.start()
    for c in copies:
        c.wait()


def join(a, b):
    return pl.pallas_call(
        join_kernel,
        in_specs=[pl.BlockSpec(memory_space=pl.ANY)] * 2,
        out_specs=WHOLE,
        out_shape=jax.ShapeDtypeStruct((2 * TOK, 128), BF16),
        scratch_shapes=[pltpu.SemaphoreType.DMA((2,))],
        compiler_params=params(2),
        name="join",
    )(a, b)


def arrange_kernel(place, *refs):
    blocks, out = refs[:4], refs[4]
    for c in range(4):
        e = lax.rem(place[3] + 4 - c, 4)
        out[jnp.where(e // 2 == place[0], 0, 1), lax.rem(e, 2)] = blocks[c][...]


def arrange(place, blocks):
    return pl.pallas_call(
        arrange_kernel,
        in_specs=[SCALARS] + [WHOLE] * 4,
        out_specs=WHOLE,
        out_shape=jax.ShapeDtypeStruct((2, 2, 2 * TOK, 128), BF16),
        compiler_params=params(8),
        name="arrange",
    )(place, *blocks)


def rows_at(place, d, s, q, crossed=False):
    first, second = (place[2], place[1]) if crossed else (place[1], place[2])
    last, mid = lax.rem(first + 4 - d, 4), lax.rem(second + 4 - s, 4)
    r = jnp.where(place[0] == (0 if crossed else 1), 4 * mid + last, 4 * last + mid)
    return pl.ds(pl.multiple_of((16 * q + r) * 128, 128), 128)


def score_kernel(place, *refs, steps, added, final):
    n = len(steps)
    chunks, (head, thead), refs = refs[:n], refs[n : n + 2], refs[n + 2 :]
    early, refs = (refs[0], refs[1:]) if added else (None, refs)
    if final:
        got, allowed, weights, tangent, stats, acc = refs
    else:
        (acc,) = refs
    spots = [rows_at(place, d, s, q) for d in steps for s, q in ORDER]
    left = jnp.concatenate([c[s, q] for c in chunks for s, q in ORDER], axis=1)
    for n in range(4):
        cols = slice(256 * n, 256 * n + 256)
        right = jnp.concatenate([head[r, cols] for r in spots], axis=0)
        turn = jnp.concatenate([thead[r, cols] for r in spots], axis=0)
        both = jnp.dot(left, right, preferred_element_type=F32)
        more = jnp.dot(left[:TOK], turn, preferred_element_type=F32)
        if added:
            both = both + early[:, cols]
        acc[:TOK, cols] = both[:TOK]
        acc[TOK:, cols] = both[TOK:] + more
    if not final:
        return
    lane = lax.broadcasted_iota(jnp.int32, (32, 128), 1)
    ticket = jnp.concatenate([allowed[...].astype(F32), jnp.zeros((8, 64), F32)], axis=1)
    ticket = jnp.transpose(jnp.concatenate([ticket, jnp.zeros((120, 256), F32)], axis=0))
    parts = []
    for r in range(0, TOK, 32):
        rows, trows = slice(r, r + 32), slice(TOK + r, TOK + r + 32)
        logit = acc[rows, :] + got[rows, :]
        tang = acc[trows, :] + got[trows, :]
        ok = jnp.concatenate([jnp.broadcast_to(ticket[rows, b : b + 1], (32, 128)) for b in range(8)], axis=1) > 0.5
        logit = jnp.where(ok, logit, NEG)
        top = jnp.max(logit, axis=1, keepdims=True)
        w = jnp.where(ok, jnp.exp(logit - top), 0.0)
        den = jnp.sum(w, axis=1, keepdims=True)
        mom = jnp.sum(w * tang, axis=1, keepdims=True)
        weights[rows, :] = w
        tangent[rows, :] = tang
        parts.append(jnp.where(lane == 0, top, jnp.where(lane == 1, den, jnp.where(lane == 2, mom, 0.0))))
    first = jnp.concatenate(parts[:4], axis=0)
    second = jnp.concatenate(parts[4:] + [jnp.zeros((64, 128), F32)], axis=0)
    stats[0:4, :] = jnp.transpose(first)[0:4, :]
    stats[4:8, :] = jnp.transpose(second)[0:4, :]


def scores(place, steps, chunks, head, thead, name, weight, early=None, late=()):
    added, final = early is not None, len(late) > 0
    operands = [place, *chunks, head, thead, *([early] if added else []), *late]
    shapes = [(TOK, COLS), (TOK, COLS), (8, 128)] if final else [(2 * TOK, COLS)]
    out = pl.pallas_call(
        functools.partial(score_kernel, steps=steps, added=added, final=final),
        in_specs=[SCALARS] + [WHOLE] * (len(operands) - 1),
        out_specs=[WHOLE] * len(shapes),
        out_shape=[jax.ShapeDtypeStruct(s, F32) for s in shapes],
        scratch_shapes=[pltpu.VMEM((2 * TOK, COLS), F32)] if final else [],
        compiler_params=params(12),
        cost_estimate=cost(weight * 6 * TOK * 4096 * COLS, weight << 20),
        name=name,
    )(*operands)
    return out if final else out[0]


def product_kernel(every, mine, weights, tangent, out):
    cols = []
    for g in range(2):
        top = every[:, 4 * g, :]
        best = jnp.max(top, axis=0, keepdims=True)
        scale = jnp.exp(top - best)
        den = jnp.sum(every[:, 4 * g + 1, :] * scale, axis=0, keepdims=True)
        mom = jnp.sum(every[:, 4 * g + 2, :] * scale, axis=0, keepdims=True)
        if g:
            real = lax.broadcasted_iota(jnp.int32, (1, 128), 1) < 64
            den = jnp.where(real, den, 1.0)
        factor = jnp.exp(mine[4 * g : 4 * g + 1, :] - best) / den
        mean = mom / den
        row = lax.broadcasted_iota(jnp.int32, (128, 128), 0)
        cols.append(jnp.transpose(jnp.where(row == 0, factor, jnp.where(row == 1, mean, 0.0))))
    both = jnp.concatenate([cols[0], cols[1][:64]], axis=0)
    for r in range(0, TOK, 32):
        rows = slice(r, r + 32)
        p = (weights[rows, :] * both[rows, 0:1]) * (tangent[rows, :] - both[rows, 1:2])
        out[rows, :] = p.astype(BF16)


def make_product(every, mine, weights, tangent):
    return pl.pallas_call(
        product_kernel,
        in_specs=[WHOLE] * 4,
        out_specs=WHOLE,
        out_shape=jax.ShapeDtypeStruct((TOK, COLS), BF16),
        compiler_params=params(16),
        name="product",
    )(every, mine, weights, tangent)


def back_kernel(place, product, head, *refs, crossed):
    outs, turned = refs[:4], refs[4]
    turned[...] = jnp.transpose(product[...].astype(F32)).astype(BF16)
    for d in (1, 3, 2, 0):
        rows = jnp.concatenate([head[rows_at(place, d, s, q, crossed), :] for s, q in ORDER], axis=0)
        term = jnp.dot(rows, turned[...], preferred_element_type=F32).astype(BF16)
        for s in range(4):
            low, high = term[256 * s : 256 * s + 128], term[256 * s + 128 : 256 * s + 256]
            outs[d][s, 0] = low[:, :128]
            outs[d][s, 1] = high[:, :128]
            outs[d][s, 2] = jnp.concatenate([low[:, 128:], high[:, 128:]], axis=1)


def back(place, product, head, crossed, name):
    return pl.pallas_call(
        functools.partial(back_kernel, crossed=crossed),
        in_specs=[SCALARS, WHOLE, WHOLE],
        out_specs=[WHOLE] * 4,
        out_shape=[jax.ShapeDtypeStruct((4, 3, 128, 128), BF16)] * 4,
        scratch_shapes=[pltpu.VMEM((COLS, TOK), BF16)],
        compiler_params=params(8),
        cost_estimate=cost(2 * TOK * 4096 * COLS, 10 << 20),
        name=name,
    )(place, product, head)


def added(terms, s, b):
    value = terms[0][s, b].astype(F32)
    for term in terms[1:]:
        value = value + term[s, b].astype(F32)
    return value.astype(BF16)


def line_sum_kernel(*refs):
    terms, out = refs[:4], refs[4]
    for s in range(4):
        for b in range(3):
            out[s, b] = added(terms, s, b)


def line_sum(terms):
    return pl.pallas_call(
        line_sum_kernel,
        in_specs=[WHOLE] * 4,
        out_specs=WHOLE,
        out_shape=jax.ShapeDtypeStruct((4, 3, 128, 128), BF16),
        compiler_params=params(10),
        name="line_sum",
    )(*terms)


def pack_kernel(place, *refs):
    terms, got, out = refs[:4], refs[4], refs[5]
    for s in range(4):
        mid = lax.rem(place[2] + 4 - s, 4)
        for t in range(2):
            half = jnp.where(place[0] == t, 0, 1)
            sums = [got[s, b] if t else added(terms, s, b) for b in range(3)]
            for q in range(2):
                tail = sums[2][:, 64 * q : 64 * q + 64]
                to = 4 * mid + 2 * half + q
                out[to, 0:128] = sums[q]
                out[to, 128:TOK] = jnp.concatenate([tail[:64], tail[64:]], axis=1)


def pack(place, terms, got):
    return pl.pallas_call(
        pack_kernel,
        in_specs=[SCALARS] + [WHOLE] * 5,
        out_specs=WHOLE,
        out_shape=jax.ShapeDtypeStruct((16, TOK, 128), BF16),
        compiler_params=params(10),
        name="pack",
    )(place, *terms, got)


def plane_sum_kernel(terms, out):
    value = terms[0].astype(F32)
    for j in range(1, 16):
        value = value + terms[j].astype(F32)
    fold = value[128:]
    out[0:128] = jnp.transpose(value[:128]).astype(BF16)
    tail = jnp.concatenate([fold[:, :64], fold[:, 64:]], axis=0)
    out[128:TOK] = jnp.transpose(tail).astype(BF16)


def plane_sum(terms):
    return pl.pallas_call(
        plane_sum_kernel,
        in_specs=[WHOLE],
        out_specs=WHOLE,
        out_shape=jax.ShapeDtypeStruct((TOK, 128), BF16),
        compiler_params=params(8),
        name="plane_sum",
    )(terms)


def outer_kernel(place, *refs):
    mine, others, p_own, p_other, out, held = refs[:4], refs[4:8], refs[8], refs[9], refs[10], refs[11]
    i = pl.program_id(0)

    @pl.when(i == 0)
    def _():
        for d in range(4):
            for s, q in ORDER:
                rows = rows_at(place, d, s, q)
                held[rows.start // 128, 0:TOK] = mine[d][s, q]
                held[rows.start // 128, TOK : 2 * TOK] = others[d][s, q]

    left = jnp.concatenate([held[4 * i + j] for j in range(4)], axis=1)
    right = jnp.concatenate([p_own[...], p_other[...]], axis=0)
    out[...] = lax.dot_general(left, right, (((0,), (0,)), ((), ())), preferred_element_type=F32).astype(BF16)


def outer(place, mine, others, p_own, p_other):
    rows = pl.BlockSpec((4, 2, TOK, 128), lambda i: (0, 0, 0, 0))
    whole = pl.BlockSpec((TOK, COLS), lambda i: (0, 0))
    return pl.pallas_call(
        outer_kernel,
        grid=(8,),
        in_specs=[SCALARS] + [rows] * 8 + [whole] * 2,
        out_specs=pl.BlockSpec((512, COLS), lambda i: (i, 0)),
        out_shape=jax.ShapeDtypeStruct((4096, COLS), BF16),
        scratch_shapes=[pltpu.VMEM((32, 2 * TOK, 128), BF16)],
        compiler_params=params(16),
        cost_estimate=cost(4 * TOK * 4096 * COLS, 12 << 20),
        name="head_outer",
    )(place, *mine, *others, p_own, p_other)


def shards(hidden, tangent_hidden, head, tangent_head, allowed):
    k, v = lax.axis_index("dp"), lax.axis_index("vocab")
    z, y, x = v // 16, (v // 4) % 4, v % 4
    place = jnp.stack([k, jnp.where(k == 1, x, y), jnp.where(k == 1, y, x), z]).astype(jnp.int32)
    rows = join(*(pltpu.with_memory_space_constraint(h, pltpu.HBM) for h in (hidden, tangent_hidden)))
    both = arrange(place, [permute(rows, start_pairs(c)) for c in range(4)])
    middle = [both] + [permute(both, mid_shift(s)) for s in (1, 2, 3)]
    head, middle[1] = lax.optimization_barrier((head, middle[1]))
    head_near = load_near(head, "load_head")
    middle[2], head_near = lax.optimization_barrier((middle[2], head_near))
    own = jnp.stack([m[0] for m in middle])
    other = jnp.stack([m[1] for m in middle])
    other1, other3, own3 = permute(other, last_shift(1)), permute(other, last_shift(-1)), permute(own, last_shift(-1))
    other2 = permute(other1, last_shift(1))
    tangent_head, _ = lax.optimization_barrier((tangent_head, other1))
    near = (head_near, load_near(tangent_head, "load_tangent"))
    early = scores(place, (0, 1), [other, other1], *near, "other_first", 0)
    own, other3, own3, early = lax.optimization_barrier((own, other3, own3, early))
    own2, own1 = permute(own3, last_shift(-1)), permute(own, last_shift(1))
    owns, others = [own, own1, own2, own3], [other, other1, other2, other3]

    sent = scores(place, (3, 2), [other3, other2], *near, "other_last", 10, early)
    got = permute(sent, swap_pairs())
    early = scores(place, (0, 3), [own, own3], *near, "own_first", 10)
    late = (got, jnp.transpose(allowed))
    early = scores(place, (2,), [own2], *near, "own_next", 0, early)
    weights, tangent, stats = scores(place, (1,), [own1], *near, "own_last", 0, early, late)
    every = lax.all_to_all(
        jnp.broadcast_to(stats[None], (64, 8, 128)), "vocab", split_axis=0, concat_axis=0, tiled=True
    )
    p_own = make_product(every, stats, weights, tangent)
    p_other = permute(p_own, swap_pairs())

    terms = back(place, p_own, head_near, False, "back_own")
    terms = list(terms)
    mine = [terms[0]] + [permute(terms[d], last_shift(-d)) for d in (1, 3, 2)]
    p_other, mine[0] = lax.optimization_barrier((p_other, mine[0]))
    across = back(place, p_other, head_near, True, "back_other")
    theirs = [across[0]] + [permute(across[d], mid_shift(-d)) for d in (1, 3, 2)]
    head_product = outer(place, owns, others, p_own, p_other)
    head_product, theirs[0] = lax.optimization_barrier((head_product, theirs[0]))
    rest = permute(line_sum(theirs), swap_pairs())
    slab = pack(place, mine, rest)
    arrived = lax.all_to_all(slab, AXES, split_axis=0, concat_axis=0, tiled=True, axis_index_groups=plane_groups())
    hidden_product = plane_sum(arrived)
    return head_product, hidden_product


def solution(mesh):
    place = P("dp", "vocab")
    return jax.shard_map(shards, mesh=mesh, in_specs=(place,) * 5, out_specs=(place, place), check_vma=False)
```

```python
import functools

import jax
import jax.numpy as jnp
from jax import lax
from jax.experimental import pallas as pl
from jax.experimental.pallas import tpu as pltpu
from jax.sharding import PartitionSpec as P

AXES = ("dp", "vocab")
SIDE = 4
TOK = 192
COLS = 1024
NEG = -1e30
WHOLE = pl.BlockSpec(memory_space=pltpu.VMEM)
SCALARS = pl.BlockSpec(memory_space=pltpu.SMEM)
ORDER = [(s, q) for s in range(4) for q in range(2)]
F32 = jnp.float32
BF16 = jnp.bfloat16


def flat(k, z, y, x):
    return k * 64 + (z % 4) * 16 + (y % 4) * 4 + x % 4


def sites():
    return [(k, z, y, x) for k in range(2) for z in range(4) for y in range(4) for x in range(4)]


def last_shift(d):
    return [(flat(k, z, y, x), flat(k, z, y, x + d) if k == 1 else flat(k, z, y + d, x)) for k, z, y, x in sites()]


def mid_shift(d):
    return [(flat(k, z, y, x), flat(k, z, y + d, x) if k == 1 else flat(k, z, y, x + d)) for k, z, y, x in sites()]


def swap_pairs():
    return [(flat(k, z, y, x), flat(1 - k, z, y, x)) for k, z, y, x in sites()]


def start_pairs(c):
    return [(flat(k, z, y, x), flat(z // 2, 2 * k + z % 2 + c, y, x)) for k, z, y, x in sites()]


def plane_groups():
    return [[flat(1, r, m, x) for m in range(4) for r in range(4)] for x in range(4)] + [
        [flat(0, r, y, m) for m in range(4) for r in range(4)] for y in range(4)
    ]


def permute(value, pairs):
    return lax.ppermute(value, AXES, pairs)


def params(mib):
    return pltpu.CompilerParams(vmem_limit_bytes=mib << 20)


def cost(flops, moved):
    return pl.CostEstimate(flops=flops, bytes_accessed=moved, transcendentals=0)


def load_kernel(a, out, sem):
    copy = pltpu.make_async_copy(a, out, sem)
    copy.start()
    copy.wait()


def load_near(a, name):
    return pl.pallas_call(
        load_kernel,
        in_specs=[pl.BlockSpec(memory_space=pl.ANY)],
        out_specs=WHOLE,
        out_shape=pltpu.VMEM(a.shape, a.dtype),
        scratch_shapes=[pltpu.SemaphoreType.DMA],
        compiler_params=params(2),
        cost_estimate=cost(0, 24 << 20),
        name=name,
    )(pltpu.with_memory_space_constraint(a, pltpu.HBM))


def join_kernel(a, b, out, sems):
    copies = [
        pltpu.make_async_copy(a, out.at[0:TOK], sems.at[0]),
        pltpu.make_async_copy(b, out.at[TOK : 2 * TOK], sems.at[1]),
    ]
    for c in copies:
        c.start()
    for c in copies:
        c.wait()


def join(a, b):
    return pl.pallas_call(
        join_kernel,
        in_specs=[pl.BlockSpec(memory_space=pl.ANY)] * 2,
        out_specs=WHOLE,
        out_shape=jax.ShapeDtypeStruct((2 * TOK, 128), BF16),
        scratch_shapes=[pltpu.SemaphoreType.DMA((2,))],
        compiler_params=params(2),
        name="join",
    )(a, b)


def arrange_kernel(place, *refs):
    blocks, out = refs[:4], refs[4]
    for c in range(4):
        e = lax.rem(place[3] + 4 - c, 4)
        out[jnp.where(e // 2 == place[0], 0, 1), lax.rem(e, 2)] = blocks[c][...]


def arrange(place, blocks):
    return pl.pallas_call(
        arrange_kernel,
        in_specs=[SCALARS] + [WHOLE] * 4,
        out_specs=WHOLE,
        out_shape=jax.ShapeDtypeStruct((2, 2, 2 * TOK, 128), BF16),
        compiler_params=params(8),
        name="arrange",
    )(place, *blocks)


def rows_at(place, d, s, q, crossed=False):
    first, second = (place[2], place[1]) if crossed else (place[1], place[2])
    last, mid = lax.rem(first + 4 - d, 4), lax.rem(second + 4 - s, 4)
    r = jnp.where(place[0] == (0 if crossed else 1), 4 * mid + last, 4 * last + mid)
    return pl.ds(pl.multiple_of((16 * q + r) * 128, 128), 128)


def score_kernel(place, *refs, steps, added, final):
    n = len(steps)
    chunks, (head, thead), refs = refs[:n], refs[n : n + 2], refs[n + 2 :]
    early, refs = (refs[0], refs[1:]) if added else (None, refs)
    if final:
        got, allowed, weights, tangent, stats, acc = refs
    else:
        (acc,) = refs
    spots = [rows_at(place, d, s, q) for d in steps for s, q in ORDER]
    left = jnp.concatenate([c[s, q] for c in chunks for s, q in ORDER], axis=1)
    for n in range(4):
        cols = slice(256 * n, 256 * n + 256)
        right = jnp.concatenate([head[r, cols] for r in spots], axis=0)
        turn = jnp.concatenate([thead[r, cols] for r in spots], axis=0)
        both = jnp.dot(left, right, preferred_element_type=F32)
        more = jnp.dot(left[:TOK], turn, preferred_element_type=F32)
        if added:
            both = both + early[:, cols]
        acc[:TOK, cols] = both[:TOK]
        acc[TOK:, cols] = both[TOK:] + more
    if not final:
        return
    lane = lax.broadcasted_iota(jnp.int32, (32, 128), 1)
    ticket = jnp.concatenate([allowed[...].astype(F32), jnp.zeros((8, 64), F32)], axis=1)
    ticket = jnp.transpose(jnp.concatenate([ticket, jnp.zeros((120, 256), F32)], axis=0))
    parts = []
    for r in range(0, TOK, 32):
        rows, trows = slice(r, r + 32), slice(TOK + r, TOK + r + 32)
        logit = acc[rows, :] + got[rows, :]
        tang = acc[trows, :] + got[trows, :]
        ok = jnp.concatenate([jnp.broadcast_to(ticket[rows, b : b + 1], (32, 128)) for b in range(8)], axis=1) > 0.5
        logit = jnp.where(ok, logit, NEG)
        top = jnp.max(logit, axis=1, keepdims=True)
        w = jnp.where(ok, jnp.exp(logit - top), 0.0)
        den = jnp.sum(w, axis=1, keepdims=True)
        mom = jnp.sum(w * tang, axis=1, keepdims=True)
        weights[rows, :] = w
        tangent[rows, :] = tang
        parts.append(jnp.where(lane == 0, top, jnp.where(lane == 1, den, jnp.where(lane == 2, mom, 0.0))))
    first = jnp.concatenate(parts[:4], axis=0)
    second = jnp.concatenate(parts[4:] + [jnp.zeros((64, 128), F32)], axis=0)
    stats[0:4, :] = jnp.transpose(first)[0:4, :]
    stats[4:8, :] = jnp.transpose(second)[0:4, :]


def scores(place, steps, chunks, head, thead, name, weight, early=None, late=()):
    added, final = early is not None, len(late) > 0
    operands = [place, *chunks, head, thead, *([early] if added else []), *late]
    shapes = [(TOK, COLS), (TOK, COLS), (8, 128)] if final else [(2 * TOK, COLS)]
    out = pl.pallas_call(
        functools.partial(score_kernel, steps=steps, added=added, final=final),
        in_specs=[SCALARS] + [WHOLE] * (len(operands) - 1),
        out_specs=[WHOLE] * len(shapes),
        out_shape=[jax.ShapeDtypeStruct(s, F32) for s in shapes],
        scratch_shapes=[pltpu.VMEM((2 * TOK, COLS), F32)] if final else [],
        compiler_params=params(12),
        cost_estimate=cost(weight * 6 * TOK * 4096 * COLS, weight << 20),
        name=name,
    )(*operands)
    return out if final else out[0]


def product_kernel(every, mine, weights, tangent, out):
    cols = []
    for g in range(2):
        top = every[:, 4 * g, :]
        best = jnp.max(top, axis=0, keepdims=True)
        scale = jnp.exp(top - best)
        den = jnp.sum(every[:, 4 * g + 1, :] * scale, axis=0, keepdims=True)
        mom = jnp.sum(every[:, 4 * g + 2, :] * scale, axis=0, keepdims=True)
        if g:
            real = lax.broadcasted_iota(jnp.int32, (1, 128), 1) < 64
            den = jnp.where(real, den, 1.0)
        factor = jnp.exp(mine[4 * g : 4 * g + 1, :] - best) / den
        mean = mom / den
        row = lax.broadcasted_iota(jnp.int32, (128, 128), 0)
        cols.append(jnp.transpose(jnp.where(row == 0, factor, jnp.where(row == 1, mean, 0.0))))
    both = jnp.concatenate([cols[0], cols[1][:64]], axis=0)
    for r in range(0, TOK, 32):
        rows = slice(r, r + 32)
        p = (weights[rows, :] * both[rows, 0:1]) * (tangent[rows, :] - both[rows, 1:2])
        out[rows, :] = p.astype(BF16)


def make_product(every, mine, weights, tangent):
    return pl.pallas_call(
        product_kernel,
        in_specs=[WHOLE] * 4,
        out_specs=WHOLE,
        out_shape=jax.ShapeDtypeStruct((TOK, COLS), BF16),
        compiler_params=params(16),
        name="product",
    )(every, mine, weights, tangent)


def back_kernel(place, product, head, *refs, crossed):
    outs, turned = refs[:4], refs[4]
    turned[...] = jnp.transpose(product[...].astype(F32)).astype(BF16)
    for d in (1, 3, 2, 0):
        rows = jnp.concatenate([head[rows_at(place, d, s, q, crossed), :] for s, q in ORDER], axis=0)
        term = jnp.dot(rows, turned[...], preferred_element_type=F32).astype(BF16)
        for s in range(4):
            low, high = term[256 * s : 256 * s + 128], term[256 * s + 128 : 256 * s + 256]
            outs[d][s, 0] = low[:, :128]
            outs[d][s, 1] = high[:, :128]
            outs[d][s, 2] = jnp.concatenate([low[:, 128:], high[:, 128:]], axis=1)


def back(place, product, head, crossed, name):
    return pl.pallas_call(
        functools.partial(back_kernel, crossed=crossed),
        in_specs=[SCALARS, WHOLE, WHOLE],
        out_specs=[WHOLE] * 4,
        out_shape=[jax.ShapeDtypeStruct((4, 3, 128, 128), BF16)] * 4,
        scratch_shapes=[pltpu.VMEM((COLS, TOK), BF16)],
        compiler_params=params(8),
        cost_estimate=cost(2 * TOK * 4096 * COLS, 10 << 20),
        name=name,
    )(place, product, head)


def added(terms, s, b):
    value = terms[0][s, b].astype(F32)
    for term in terms[1:]:
        value = value + term[s, b].astype(F32)
    return value.astype(BF16)


def line_sum_kernel(*refs):
    terms, out = refs[:4], refs[4]
    for s in range(4):
        for b in range(3):
            out[s, b] = added(terms, s, b)


def line_sum(terms):
    return pl.pallas_call(
        line_sum_kernel,
        in_specs=[WHOLE] * 4,
        out_specs=WHOLE,
        out_shape=jax.ShapeDtypeStruct((4, 3, 128, 128), BF16),
        compiler_params=params(10),
        name="line_sum",
    )(*terms)


def pack_kernel(place, *refs):
    terms, got, out = refs[:4], refs[4], refs[5]
    for s in range(4):
        mid = lax.rem(place[2] + 4 - s, 4)
        for t in range(2):
            half = jnp.where(place[0] == t, 0, 1)
            sums = [got[s, b] if t else added(terms, s, b) for b in range(3)]
            for q in range(2):
                tail = sums[2][:, 64 * q : 64 * q + 64]
                to = 4 * mid + 2 * half + q
                out[to, 0:128] = sums[q]
                out[to, 128:TOK] = jnp.concatenate([tail[:64], tail[64:]], axis=1)


def pack(place, terms, got):
    return pl.pallas_call(
        pack_kernel,
        in_specs=[SCALARS] + [WHOLE] * 5,
        out_specs=WHOLE,
        out_shape=jax.ShapeDtypeStruct((16, TOK, 128), BF16),
        compiler_params=params(10),
        name="pack",
    )(place, *terms, got)


def plane_sum_kernel(terms, out):
    value = terms[0].astype(F32)
    for j in range(1, 16):
        value = value + terms[j].astype(F32)
    fold = value[128:]
    out[0:128] = jnp.transpose(value[:128]).astype(BF16)
    tail = jnp.concatenate([fold[:, :64], fold[:, 64:]], axis=0)
    out[128:TOK] = jnp.transpose(tail).astype(BF16)


def plane_sum(terms):
    return pl.pallas_call(
        plane_sum_kernel,
        in_specs=[WHOLE],
        out_specs=WHOLE,
        out_shape=jax.ShapeDtypeStruct((TOK, 128), BF16),
        compiler_params=params(8),
        name="plane_sum",
    )(terms)


def outer_kernel(place, *refs):
    mine, others, p_own, p_other, out, held = refs[:4], refs[4:8], refs[8], refs[9], refs[10], refs[11]
    i = pl.program_id(0)

    @pl.when(i == 0)
    def _():
        for d in range(4):
            for s, q in ORDER:
                rows = rows_at(place, d, s, q)
                held[rows.start // 128, 0:TOK] = mine[d][s, q]
                held[rows.start // 128, TOK : 2 * TOK] = others[d][s, q]

    left = jnp.concatenate([held[4 * i + j] for j in range(4)], axis=1)
    right = jnp.concatenate([p_own[...], p_other[...]], axis=0)
    out[...] = lax.dot_general(left, right, (((0,), (0,)), ((), ())), preferred_element_type=F32).astype(BF16)


def outer(place, mine, others, p_own, p_other):
    rows = pl.BlockSpec((4, 2, TOK, 128), lambda i: (0, 0, 0, 0))
    whole = pl.BlockSpec((TOK, COLS), lambda i: (0, 0))
    return pl.pallas_call(
        outer_kernel,
        grid=(8,),
        in_specs=[SCALARS] + [rows] * 8 + [whole] * 2,
        out_specs=pl.BlockSpec((512, COLS), lambda i: (i, 0)),
        out_shape=jax.ShapeDtypeStruct((4096, COLS), BF16),
        scratch_shapes=[pltpu.VMEM((32, 2 * TOK, 128), BF16)],
        compiler_params=params(16),
        cost_estimate=cost(4 * TOK * 4096 * COLS, 12 << 20),
        name="head_outer",
    )(place, *mine, *others, p_own, p_other)


def shards(hidden, tangent_hidden, head, tangent_head, allowed):
    k, v = lax.axis_index("dp"), lax.axis_index("vocab")
    z, y, x = v // 16, (v // 4) % 4, v % 4
    place = jnp.stack([k, jnp.where(k == 1, x, y), jnp.where(k == 1, y, x), z]).astype(jnp.int32)
    rows = join(*(pltpu.with_memory_space_constraint(h, pltpu.HBM) for h in (hidden, tangent_hidden)))
    both = arrange(place, [permute(rows, start_pairs(c)) for c in range(4)])
    middle = [both] + [permute(both, mid_shift(s)) for s in (1, 2, 3)]
    head, middle[1] = lax.optimization_barrier((head, middle[1]))
    head_near = load_near(head, "load_head")
    middle[2], head_near = lax.optimization_barrier((middle[2], head_near))
    own = jnp.stack([m[0] for m in middle])
    other = jnp.stack([m[1] for m in middle])
    other1, other3, own3 = permute(other, last_shift(1)), permute(other, last_shift(-1)), permute(own, last_shift(-1))
    other2 = permute(other1, last_shift(1))
    tangent_head, _ = lax.optimization_barrier((tangent_head, other1))
    near = (head_near, load_near(tangent_head, "load_tangent"))
    early = scores(place, (0, 1), [other, other1], *near, "other_first", 0)
    own, other3, own3, early = lax.optimization_barrier((own, other3, own3, early))
    own2, own1 = permute(own3, last_shift(-1)), permute(own, last_shift(1))
    owns, others = [own, own1, own2, own3], [other, other1, other2, other3]

    sent = scores(place, (3, 2), [other3, other2], *near, "other_last", 10, early)
    got = permute(sent, swap_pairs())
    early = scores(place, (0, 3), [own, own3], *near, "own_first", 10)
    late = (got, jnp.transpose(allowed))
    early = scores(place, (2,), [own2], *near, "own_next", 0, early)
    weights, tangent, stats = scores(place, (1,), [own1], *near, "own_last", 0, early, late)
    every = lax.all_to_all(
        jnp.broadcast_to(stats[None], (64, 8, 128)), "vocab", split_axis=0, concat_axis=0, tiled=True
    )
    p_own = make_product(every, stats, weights, tangent)
    p_other = permute(p_own, swap_pairs())

    terms = back(place, p_own, head_near, False, "back_own")
    mine = [terms[0]] + [permute(terms[d], last_shift(-d)) for d in (1, 3)]
    across = back(place, p_other, head_near, True, "back_other")
    theirs = [across[0]] + [permute(across[d], mid_shift(-d)) for d in (1, 3, 2)]
    term, _ = lax.optimization_barrier((terms[2], across[0]))
    mine.append(permute(term, last_shift(-2)))
    p_own, theirs[1] = lax.optimization_barrier((p_own, theirs[1]))
    head_product = outer(place, owns, others, p_own, p_other)
    head_product, theirs[0] = lax.optimization_barrier((head_product, theirs[0]))
    rest = permute(line_sum(theirs), swap_pairs())
    slab = pack(place, mine, rest)
    arrived = lax.all_to_all(slab, AXES, split_axis=0, concat_axis=0, tiled=True, axis_index_groups=plane_groups())
    hidden_product = plane_sum(arrived)
    return head_product, hidden_product


def solution(mesh):
    place = P("dp", "vocab")
    return jax.shard_map(shards, mesh=mesh, in_specs=(place,) * 5, out_specs=(place, place), check_vma=False)
```

```python
import functools

import jax
import jax.numpy as jnp
from jax import lax
from jax.experimental import pallas as pl
from jax.experimental.pallas import tpu as pltpu
from jax.sharding import PartitionSpec as P

AXES = ("dp", "vocab")
SIDE = 4
TOK = 192
COLS = 1024
NEG = -1e30
WHOLE = pl.BlockSpec(memory_space=pltpu.VMEM)
SCALARS = pl.BlockSpec(memory_space=pltpu.SMEM)
ORDER = [(s, q) for s in range(4) for q in range(2)]
F32 = jnp.float32
BF16 = jnp.bfloat16


def flat(k, z, y, x):
    return k * 64 + (z % 4) * 16 + (y % 4) * 4 + x % 4


def sites():
    return [(k, z, y, x) for k in range(2) for z in range(4) for y in range(4) for x in range(4)]


def last_shift(d):
    return [(flat(k, z, y, x), flat(k, z, y, x + d) if k == 1 else flat(k, z, y + d, x)) for k, z, y, x in sites()]


def mid_shift(d):
    return [(flat(k, z, y, x), flat(k, z, y + d, x) if k == 1 else flat(k, z, y, x + d)) for k, z, y, x in sites()]


def swap_pairs():
    return [(flat(k, z, y, x), flat(1 - k, z, y, x)) for k, z, y, x in sites()]


def start_pairs(c):
    return [(flat(k, z, y, x), flat(z // 2, 2 * k + z % 2 + c, y, x)) for k, z, y, x in sites()]


def plane_groups():
    return [[flat(1, r, m, x) for m in range(4) for r in range(4)] for x in range(4)] + [
        [flat(0, r, y, m) for m in range(4) for r in range(4)] for y in range(4)
    ]


def permute(value, pairs):
    return lax.ppermute(value, AXES, pairs)


def params(mib):
    return pltpu.CompilerParams(vmem_limit_bytes=mib << 20)


def cost(flops, moved):
    return pl.CostEstimate(flops=flops, bytes_accessed=moved, transcendentals=0)


def load_kernel(a, out, sem):
    copy = pltpu.make_async_copy(a, out, sem)
    copy.start()
    copy.wait()


def load_near(a, name):
    return pl.pallas_call(
        load_kernel,
        in_specs=[pl.BlockSpec(memory_space=pl.ANY)],
        out_specs=WHOLE,
        out_shape=pltpu.VMEM(a.shape, a.dtype),
        scratch_shapes=[pltpu.SemaphoreType.DMA],
        compiler_params=params(2),
        cost_estimate=cost(0, 24 << 20),
        name=name,
    )(pltpu.with_memory_space_constraint(a, pltpu.HBM))


def join_kernel(a, b, out, sems):
    copies = [
        pltpu.make_async_copy(a, out.at[0:TOK], sems.at[0]),
        pltpu.make_async_copy(b, out.at[TOK : 2 * TOK], sems.at[1]),
    ]
    for c in copies:
        c.start()
    for c in copies:
        c.wait()


def join(a, b):
    return pl.pallas_call(
        join_kernel,
        in_specs=[pl.BlockSpec(memory_space=pl.ANY)] * 2,
        out_specs=WHOLE,
        out_shape=jax.ShapeDtypeStruct((2 * TOK, 128), BF16),
        scratch_shapes=[pltpu.SemaphoreType.DMA((2,))],
        compiler_params=params(2),
        name="join",
    )(a, b)


def arrange_kernel(place, *refs):
    blocks, out = refs[:4], refs[4]
    for c in range(4):
        e = lax.rem(place[3] + 4 - c, 4)
        out[jnp.where(e // 2 == place[0], 0, 1), lax.rem(e, 2)] = blocks[c][...]


def arrange(place, blocks):
    return pl.pallas_call(
        arrange_kernel,
        in_specs=[SCALARS] + [WHOLE] * 4,
        out_specs=WHOLE,
        out_shape=jax.ShapeDtypeStruct((2, 2, 2 * TOK, 128), BF16),
        compiler_params=params(8),
        name="arrange",
    )(place, *blocks)


def rows_at(place, d, s, q, crossed=False):
    first, second = (place[2], place[1]) if crossed else (place[1], place[2])
    last, mid = lax.rem(first + 4 - d, 4), lax.rem(second + 4 - s, 4)
    r = jnp.where(place[0] == (0 if crossed else 1), 4 * mid + last, 4 * last + mid)
    return pl.ds(pl.multiple_of((16 * q + r) * 128, 128), 128)


def score_kernel(place, *refs, steps, added, final):
    n = len(steps)
    chunks, (head, thead), refs = refs[:n], refs[n : n + 2], refs[n + 2 :]
    early, refs = (refs[0], refs[1:]) if added else (None, refs)
    if final:
        got, allowed, weights, tangent, stats, acc = refs
    else:
        (acc,) = refs
    spots = [rows_at(place, d, s, q) for d in steps for s, q in ORDER]
    left = jnp.concatenate([c[s, q] for c in chunks for s, q in ORDER], axis=1)
    for n in range(4):
        cols = slice(256 * n, 256 * n + 256)
        right = jnp.concatenate([head[r, cols] for r in spots], axis=0)
        turn = jnp.concatenate([thead[r, cols] for r in spots], axis=0)
        both = jnp.dot(left, right, preferred_element_type=F32)
        more = jnp.dot(left[:TOK], turn, preferred_element_type=F32)
        if added:
            both = both + early[:, cols]
        acc[:TOK, cols] = both[:TOK]
        acc[TOK:, cols] = both[TOK:] + more
    if not final:
        return
    lane = lax.broadcasted_iota(jnp.int32, (32, 128), 1)
    ticket = jnp.concatenate([allowed[...].astype(F32), jnp.zeros((8, 64), F32)], axis=1)
    ticket = jnp.transpose(jnp.concatenate([ticket, jnp.zeros((120, 256), F32)], axis=0))
    parts = []
    for r in range(0, TOK, 32):
        rows, trows = slice(r, r + 32), slice(TOK + r, TOK + r + 32)
        logit = acc[rows, :] + got[rows, :]
        tang = acc[trows, :] + got[trows, :]
        ok = jnp.concatenate([jnp.broadcast_to(ticket[rows, b : b + 1], (32, 128)) for b in range(8)], axis=1) > 0.5
        logit = jnp.where(ok, logit, NEG)
        top = jnp.max(logit, axis=1, keepdims=True)
        w = jnp.where(ok, jnp.exp(logit - top), 0.0)
        den = jnp.sum(w, axis=1, keepdims=True)
        mom = jnp.sum(w * tang, axis=1, keepdims=True)
        weights[rows, :] = w
        tangent[rows, :] = tang
        parts.append(jnp.where(lane == 0, top, jnp.where(lane == 1, den, jnp.where(lane == 2, mom, 0.0))))
    first = jnp.concatenate(parts[:4], axis=0)
    second = jnp.concatenate(parts[4:] + [jnp.zeros((64, 128), F32)], axis=0)
    stats[0:4, :] = jnp.transpose(first)[0:4, :]
    stats[4:8, :] = jnp.transpose(second)[0:4, :]


def scores(place, steps, chunks, head, thead, name, weight, early=None, late=()):
    added, final = early is not None, len(late) > 0
    operands = [place, *chunks, head, thead, *([early] if added else []), *late]
    shapes = [(TOK, COLS), (TOK, COLS), (8, 128)] if final else [(2 * TOK, COLS)]
    out = pl.pallas_call(
        functools.partial(score_kernel, steps=steps, added=added, final=final),
        in_specs=[SCALARS] + [WHOLE] * (len(operands) - 1),
        out_specs=[WHOLE] * len(shapes),
        out_shape=[jax.ShapeDtypeStruct(s, F32) for s in shapes],
        scratch_shapes=[pltpu.VMEM((2 * TOK, COLS), F32)] if final else [],
        compiler_params=params(12),
        cost_estimate=cost(weight * 6 * TOK * 4096 * COLS, weight << 20),
        name=name,
    )(*operands)
    return out if final else out[0]


def product_kernel(every, mine, weights, tangent, out):
    cols = []
    for g in range(2):
        top = every[:, 4 * g, :]
        best = jnp.max(top, axis=0, keepdims=True)
        scale = jnp.exp(top - best)
        den = jnp.sum(every[:, 4 * g + 1, :] * scale, axis=0, keepdims=True)
        mom = jnp.sum(every[:, 4 * g + 2, :] * scale, axis=0, keepdims=True)
        if g:
            real = lax.broadcasted_iota(jnp.int32, (1, 128), 1) < 64
            den = jnp.where(real, den, 1.0)
        factor = jnp.exp(mine[4 * g : 4 * g + 1, :] - best) / den
        mean = mom / den
        row = lax.broadcasted_iota(jnp.int32, (128, 128), 0)
        cols.append(jnp.transpose(jnp.where(row == 0, factor, jnp.where(row == 1, mean, 0.0))))
    both = jnp.concatenate([cols[0], cols[1][:64]], axis=0)
    for r in range(0, TOK, 32):
        rows = slice(r, r + 32)
        p = (weights[rows, :] * both[rows, 0:1]) * (tangent[rows, :] - both[rows, 1:2])
        out[rows, :] = p.astype(BF16)


def make_product(every, mine, weights, tangent):
    return pl.pallas_call(
        product_kernel,
        in_specs=[WHOLE] * 4,
        out_specs=WHOLE,
        out_shape=jax.ShapeDtypeStruct((TOK, COLS), BF16),
        compiler_params=params(16),
        name="product",
    )(every, mine, weights, tangent)


def back_kernel(place, product, head, *refs, crossed):
    outs, turned = refs[:4], refs[4]
    turned[...] = jnp.transpose(product[...].astype(F32)).astype(BF16)
    for d in (1, 3, 2, 0):
        rows = jnp.concatenate([head[rows_at(place, d, s, q, crossed), :] for s, q in ORDER], axis=0)
        term = jnp.dot(rows, turned[...], preferred_element_type=F32).astype(BF16)
        for s in range(4):
            low, high = term[256 * s : 256 * s + 128], term[256 * s + 128 : 256 * s + 256]
            outs[d][s, 0] = low[:, :128]
            outs[d][s, 1] = high[:, :128]
            outs[d][s, 2] = jnp.concatenate([low[:, 128:], high[:, 128:]], axis=1)


def back(place, product, head, crossed, name):
    return pl.pallas_call(
        functools.partial(back_kernel, crossed=crossed),
        in_specs=[SCALARS, WHOLE, WHOLE],
        out_specs=[WHOLE] * 4,
        out_shape=[jax.ShapeDtypeStruct((4, 3, 128, 128), BF16)] * 4,
        scratch_shapes=[pltpu.VMEM((COLS, TOK), BF16)],
        compiler_params=params(8),
        cost_estimate=cost(2 * TOK * 4096 * COLS, 10 << 20),
        name=name,
    )(place, product, head)


def added(terms, s, b):
    value = terms[0][s, b].astype(F32)
    for term in terms[1:]:
        value = value + term[s, b].astype(F32)
    return value.astype(BF16)


def line_sum_kernel(*refs):
    terms, out = refs[:4], refs[4]
    for s in range(4):
        for b in range(3):
            out[s, b] = added(terms, s, b)


def line_sum(terms):
    return pl.pallas_call(
        line_sum_kernel,
        in_specs=[WHOLE] * 4,
        out_specs=WHOLE,
        out_shape=jax.ShapeDtypeStruct((4, 3, 128, 128), BF16),
        compiler_params=params(10),
        name="line_sum",
    )(*terms)


def pack_kernel(place, *refs):
    terms, got, out = refs[:4], refs[4], refs[5]
    for s in range(4):
        mid = lax.rem(place[2] + 4 - s, 4)
        for t in range(2):
            half = jnp.where(place[0] == t, 0, 1)
            sums = [got[s, b] if t else added(terms, s, b) for b in range(3)]
            for q in range(2):
                tail = sums[2][:, 64 * q : 64 * q + 64]
                to = 4 * mid + 2 * half + q
                out[to, 0:128] = sums[q]
                out[to, 128:TOK] = jnp.concatenate([tail[:64], tail[64:]], axis=1)


def pack(place, terms, got):
    return pl.pallas_call(
        pack_kernel,
        in_specs=[SCALARS] + [WHOLE] * 5,
        out_specs=WHOLE,
        out_shape=jax.ShapeDtypeStruct((16, TOK, 128), BF16),
        compiler_params=params(10),
        name="pack",
    )(place, *terms, got)


def plane_sum_kernel(terms, out):
    value = terms[0].astype(F32)
    for j in range(1, 16):
        value = value + terms[j].astype(F32)
    fold = value[128:]
    out[0:128] = jnp.transpose(value[:128]).astype(BF16)
    tail = jnp.concatenate([fold[:, :64], fold[:, 64:]], axis=0)
    out[128:TOK] = jnp.transpose(tail).astype(BF16)


def plane_sum(terms):
    return pl.pallas_call(
        plane_sum_kernel,
        in_specs=[WHOLE],
        out_specs=WHOLE,
        out_shape=jax.ShapeDtypeStruct((TOK, 128), BF16),
        compiler_params=params(8),
        name="plane_sum",
    )(terms)


def outer_kernel(place, *refs):
    mine, others, p_own, p_other, out, held = refs[:4], refs[4:8], refs[8], refs[9], refs[10], refs[11]
    i = pl.program_id(0)

    @pl.when(i == 0)
    def _():
        for d in range(4):
            for s, q in ORDER:
                rows = rows_at(place, d, s, q)
                held[rows.start // 128, 0:TOK] = mine[d][s, q]
                held[rows.start // 128, TOK : 2 * TOK] = others[d][s, q]

    left = jnp.concatenate([held[4 * i + j] for j in range(4)], axis=1)
    right = jnp.concatenate([p_own[...], p_other[...]], axis=0)
    out[...] = lax.dot_general(left, right, (((0,), (0,)), ((), ())), preferred_element_type=F32).astype(BF16)


def outer(place, mine, others, p_own, p_other):
    rows = pl.BlockSpec((4, 2, TOK, 128), lambda i: (0, 0, 0, 0))
    whole = pl.BlockSpec((TOK, COLS), lambda i: (0, 0))
    return pl.pallas_call(
        outer_kernel,
        grid=(8,),
        in_specs=[SCALARS] + [rows] * 8 + [whole] * 2,
        out_specs=pl.BlockSpec((512, COLS), lambda i: (i, 0)),
        out_shape=jax.ShapeDtypeStruct((4096, COLS), BF16),
        scratch_shapes=[pltpu.VMEM((32, 2 * TOK, 128), BF16)],
        compiler_params=params(16),
        cost_estimate=cost(4 * TOK * 4096 * COLS, 12 << 20),
        name="head_outer",
    )(place, *mine, *others, p_own, p_other)


def shards(hidden, tangent_hidden, head, tangent_head, allowed):
    k, v = lax.axis_index("dp"), lax.axis_index("vocab")
    z, y, x = v // 16, (v // 4) % 4, v % 4
    place = jnp.stack([k, jnp.where(k == 1, x, y), jnp.where(k == 1, y, x), z]).astype(jnp.int32)
    rows = join(*(pltpu.with_memory_space_constraint(h, pltpu.HBM) for h in (hidden, tangent_hidden)))
    both = arrange(place, [permute(rows, start_pairs(c)) for c in range(4)])
    middle = [both] + [permute(both, mid_shift(s)) for s in (1, 2, 3)]
    head, middle[1] = lax.optimization_barrier((head, middle[1]))
    head_near = load_near(head, "load_head")
    middle[2], head_near = lax.optimization_barrier((middle[2], head_near))
    own = jnp.stack([m[0] for m in middle])
    other = jnp.stack([m[1] for m in middle])
    other1, other3, own3 = permute(other, last_shift(1)), permute(other, last_shift(-1)), permute(own, last_shift(-1))
    other2 = permute(other1, last_shift(1))
    tangent_head, _ = lax.optimization_barrier((tangent_head, other1))
    near = (head_near, load_near(tangent_head, "load_tangent"))
    early = scores(place, (0, 1), [other, other1], *near, "other_first", 0)
    own, early = lax.optimization_barrier((own, early))
    own1, own2 = permute(own, last_shift(1)), permute(own3, last_shift(-1))
    owns, others = [own, own1, own2, own3], [other, other1, other2, other3]

    sent = scores(place, (3, 2), [other3, other2], *near, "other_last", 10, early)
    got = permute(sent, swap_pairs())
    early = scores(place, (0, 3), [own, own3], *near, "own_first", 10)
    late = (got, jnp.transpose(allowed))
    early = scores(place, (1,), [own1], *near, "own_next", 0, early)
    weights, tangent, stats = scores(place, (2,), [own2], *near, "own_last", 0, early, late)
    every = lax.all_to_all(
        jnp.broadcast_to(stats[None], (64, 8, 128)), "vocab", split_axis=0, concat_axis=0, tiled=True
    )
    p_own = make_product(every, stats, weights, tangent)
    p_other = permute(p_own, swap_pairs())

    terms = back(place, p_own, head_near, False, "back_own")
    mine = [terms[0]] + [permute(terms[d], last_shift(-d)) for d in (1, 3)]
    across = back(place, p_other, head_near, True, "back_other")
    theirs = [across[0]] + [permute(across[d], mid_shift(-d)) for d in (1, 3, 2)]
    term, _ = lax.optimization_barrier((terms[2], across[0]))
    mine.append(permute(term, last_shift(-2)))
    p_own, theirs[1] = lax.optimization_barrier((p_own, theirs[1]))
    head_product = outer(place, owns, others, p_own, p_other)
    head_product, theirs[0] = lax.optimization_barrier((head_product, theirs[0]))
    rest = permute(line_sum(theirs), swap_pairs())
    slab = pack(place, mine, rest)
    arrived = lax.all_to_all(slab, AXES, split_axis=0, concat_axis=0, tiled=True, axis_index_groups=plane_groups())
    hidden_product = plane_sum(arrived)
    return head_product, hidden_product


def solution(mesh):
    place = P("dp", "vocab")
    return jax.shard_map(shards, mesh=mesh, in_specs=(place,) * 5, out_specs=(place, place), check_vma=False)
```

```python
import functools

import jax
import jax.numpy as jnp
from jax import lax
from jax.experimental import pallas as pl
from jax.experimental.pallas import tpu as pltpu
from jax.sharding import PartitionSpec as P

AXES = ("dp", "vocab")
SIDE = 4
TOK = 192
COLS = 1024
NEG = -1e30
WHOLE = pl.BlockSpec(memory_space=pltpu.VMEM)
SCALARS = pl.BlockSpec(memory_space=pltpu.SMEM)
ORDER = [(s, q) for s in range(4) for q in range(2)]
F32 = jnp.float32
BF16 = jnp.bfloat16


def flat(k, z, y, x):
    return k * 64 + (z % 4) * 16 + (y % 4) * 4 + x % 4


def sites():
    return [(k, z, y, x) for k in range(2) for z in range(4) for y in range(4) for x in range(4)]


def last_shift(d):
    return [(flat(k, z, y, x), flat(k, z, y, x + d) if k == 1 else flat(k, z, y + d, x)) for k, z, y, x in sites()]


def mid_shift(d):
    return [(flat(k, z, y, x), flat(k, z, y + d, x) if k == 1 else flat(k, z, y, x + d)) for k, z, y, x in sites()]


def swap_pairs():
    return [(flat(k, z, y, x), flat(1 - k, z, y, x)) for k, z, y, x in sites()]


def start_pairs(c):
    return [(flat(k, z, y, x), flat(z // 2, 2 * k + z % 2 + c, y, x)) for k, z, y, x in sites()]


def plane_groups():
    return [[flat(1, r, m, x) for m in range(4) for r in range(4)] for x in range(4)] + [
        [flat(0, r, y, m) for m in range(4) for r in range(4)] for y in range(4)
    ]


def permute(value, pairs):
    return lax.ppermute(value, AXES, pairs)


def params(mib):
    return pltpu.CompilerParams(vmem_limit_bytes=mib << 20)


def cost(flops, moved):
    return pl.CostEstimate(flops=flops, bytes_accessed=moved, transcendentals=0)


def load_kernel(a, out, sem):
    copy = pltpu.make_async_copy(a, out, sem)
    copy.start()
    copy.wait()


def load_near(a, name):
    return pl.pallas_call(
        load_kernel,
        in_specs=[pl.BlockSpec(memory_space=pl.ANY)],
        out_specs=WHOLE,
        out_shape=pltpu.VMEM(a.shape, a.dtype),
        scratch_shapes=[pltpu.SemaphoreType.DMA],
        compiler_params=params(2),
        cost_estimate=cost(0, 24 << 20),
        name=name,
    )(pltpu.with_memory_space_constraint(a, pltpu.HBM))


def join_kernel(a, b, out, sems):
    copies = [
        pltpu.make_async_copy(a, out.at[0:TOK], sems.at[0]),
        pltpu.make_async_copy(b, out.at[TOK : 2 * TOK], sems.at[1]),
    ]
    for c in copies:
        c.start()
    for c in copies:
        c.wait()


def join(a, b):
    return pl.pallas_call(
        join_kernel,
        in_specs=[pl.BlockSpec(memory_space=pl.ANY)] * 2,
        out_specs=WHOLE,
        out_shape=jax.ShapeDtypeStruct((2 * TOK, 128), BF16),
        scratch_shapes=[pltpu.SemaphoreType.DMA((2,))],
        compiler_params=params(2),
        name="join",
    )(a, b)


def arrange_kernel(place, *refs):
    blocks, out = refs[:4], refs[4]
    for c in range(4):
        e = lax.rem(place[3] + 4 - c, 4)
        out[jnp.where(e // 2 == place[0], 0, 1), lax.rem(e, 2)] = blocks[c][...]


def arrange(place, blocks):
    return pl.pallas_call(
        arrange_kernel,
        in_specs=[SCALARS] + [WHOLE] * 4,
        out_specs=WHOLE,
        out_shape=jax.ShapeDtypeStruct((2, 2, 2 * TOK, 128), BF16),
        compiler_params=params(8),
        name="arrange",
    )(place, *blocks)


def rows_at(place, d, s, q, crossed=False):
    first, second = (place[2], place[1]) if crossed else (place[1], place[2])
    last, mid = lax.rem(first + 4 - d, 4), lax.rem(second + 4 - s, 4)
    r = jnp.where(place[0] == (0 if crossed else 1), 4 * mid + last, 4 * last + mid)
    return pl.ds(pl.multiple_of((16 * q + r) * 128, 128), 128)


def score_kernel(place, *refs, steps, added, final):
    n = len(steps)
    chunks, (head, thead), refs = refs[:n], refs[n : n + 2], refs[n + 2 :]
    early, refs = (refs[0], refs[1:]) if added else (None, refs)
    if final:
        got, allowed, weights, tangent, stats, acc = refs
    else:
        (acc,) = refs
    spots = [rows_at(place, d, s, q) for d in steps for s, q in ORDER]
    left = jnp.concatenate([c[s, q] for c in chunks for s, q in ORDER], axis=1)
    for n in range(4):
        cols = slice(256 * n, 256 * n + 256)
        right = jnp.concatenate([head[r, cols] for r in spots], axis=0)
        turn = jnp.concatenate([thead[r, cols] for r in spots], axis=0)
        both = jnp.dot(left, right, preferred_element_type=F32)
        more = jnp.dot(left[:TOK], turn, preferred_element_type=F32)
        if added:
            both = both + early[:, cols]
        acc[:TOK, cols] = both[:TOK]
        acc[TOK:, cols] = both[TOK:] + more
    if not final:
        return
    lane = lax.broadcasted_iota(jnp.int32, (32, 128), 1)
    ticket = jnp.concatenate([allowed[...].astype(F32), jnp.zeros((8, 64), F32)], axis=1)
    ticket = jnp.transpose(jnp.concatenate([ticket, jnp.zeros((120, 256), F32)], axis=0))
    parts = []
    for r in range(0, TOK, 32):
        rows, trows = slice(r, r + 32), slice(TOK + r, TOK + r + 32)
        logit = acc[rows, :] + got[rows, :]
        tang = acc[trows, :] + got[trows, :]
        ok = jnp.concatenate([jnp.broadcast_to(ticket[rows, b : b + 1], (32, 128)) for b in range(8)], axis=1) > 0.5
        logit = jnp.where(ok, logit, NEG)
        top = jnp.max(logit, axis=1, keepdims=True)
        w = jnp.where(ok, jnp.exp(logit - top), 0.0)
        den = jnp.sum(w, axis=1, keepdims=True)
        mom = jnp.sum(w * tang, axis=1, keepdims=True)
        weights[rows, :] = w
        tangent[rows, :] = tang
        parts.append(jnp.where(lane == 0, top, jnp.where(lane == 1, den, jnp.where(lane == 2, mom, 0.0))))
    first = jnp.concatenate(parts[:4], axis=0)
    second = jnp.concatenate(parts[4:] + [jnp.zeros((64, 128), F32)], axis=0)
    stats[0:4, :] = jnp.transpose(first)[0:4, :]
    stats[4:8, :] = jnp.transpose(second)[0:4, :]


def scores(place, steps, chunks, head, thead, name, weight, early=None, late=()):
    added, final = early is not None, len(late) > 0
    operands = [place, *chunks, head, thead, *([early] if added else []), *late]
    shapes = [(TOK, COLS), (TOK, COLS), (8, 128)] if final else [(2 * TOK, COLS)]
    out = pl.pallas_call(
        functools.partial(score_kernel, steps=steps, added=added, final=final),
        in_specs=[SCALARS] + [WHOLE] * (len(operands) - 1),
        out_specs=[WHOLE] * len(shapes),
        out_shape=[jax.ShapeDtypeStruct(s, F32) for s in shapes],
        scratch_shapes=[pltpu.VMEM((2 * TOK, COLS), F32)] if final else [],
        compiler_params=params(12),
        cost_estimate=cost(weight * 6 * TOK * 4096 * COLS, weight << 20),
        name=name,
    )(*operands)
    return out if final else out[0]


def product_kernel(every, mine, weights, tangent, out, turned):
    cols = []
    for g in range(2):
        top = every[:, 4 * g, :]
        best = jnp.max(top, axis=0, keepdims=True)
        scale = jnp.exp(top - best)
        den = jnp.sum(every[:, 4 * g + 1, :] * scale, axis=0, keepdims=True)
        mom = jnp.sum(every[:, 4 * g + 2, :] * scale, axis=0, keepdims=True)
        if g:
            real = lax.broadcasted_iota(jnp.int32, (1, 128), 1) < 64
            den = jnp.where(real, den, 1.0)
        factor = jnp.exp(mine[4 * g : 4 * g + 1, :] - best) / den
        mean = mom / den
        row = lax.broadcasted_iota(jnp.int32, (128, 128), 0)
        cols.append(jnp.transpose(jnp.where(row == 0, factor, jnp.where(row == 1, mean, 0.0))))
    both = jnp.concatenate([cols[0], cols[1][:64]], axis=0)
    for r in range(0, TOK, 32):
        rows = slice(r, r + 32)
        p = (weights[rows, :] * both[rows, 0:1]) * (tangent[rows, :] - both[rows, 1:2])
        out[rows, :] = p.astype(BF16)
    turned[...] = jnp.transpose(out[...].astype(F32)).astype(BF16)


def make_product(every, mine, weights, tangent):
    return pl.pallas_call(
        product_kernel,
        in_specs=[WHOLE] * 4,
        out_specs=[WHOLE] * 2,
        out_shape=[jax.ShapeDtypeStruct((TOK, COLS), BF16), jax.ShapeDtypeStruct((COLS, TOK), BF16)],
        compiler_params=params(16),
        name="product",
    )(every, mine, weights, tangent)


def back_kernel(place, turned, head, *outs, crossed):
    for d in (1, 3, 2, 0):
        rows = jnp.concatenate([head[rows_at(place, d, s, q, crossed), :] for s, q in ORDER], axis=0)
        term = jnp.dot(rows, turned[...], preferred_element_type=F32).astype(BF16)
        for s in range(4):
            low, high = term[256 * s : 256 * s + 128], term[256 * s + 128 : 256 * s + 256]
            outs[d][s, 0] = low[:, :128]
            outs[d][s, 1] = high[:, :128]
            outs[d][s, 2] = jnp.concatenate([low[:, 128:], high[:, 128:]], axis=1)


def back(place, turned, head, crossed, name):
    return pl.pallas_call(
        functools.partial(back_kernel, crossed=crossed),
        in_specs=[SCALARS, WHOLE, WHOLE],
        out_specs=[WHOLE] * 4,
        out_shape=[jax.ShapeDtypeStruct((4, 3, 128, 128), BF16)] * 4,
        compiler_params=params(8),
        cost_estimate=cost(2 * TOK * 4096 * COLS, 10 << 20),
        name=name,
    )(place, turned, head)


def added(terms, s, b):
    value = terms[0][s, b].astype(F32)
    for term in terms[1:]:
        value = value + term[s, b].astype(F32)
    return value.astype(BF16)


def line_sum_kernel(*refs):
    terms, out = refs[:4], refs[4]
    for s in range(4):
        for b in range(3):
            out[s, b] = added(terms, s, b)


def line_sum(terms):
    return pl.pallas_call(
        line_sum_kernel,
        in_specs=[WHOLE] * 4,
        out_specs=WHOLE,
        out_shape=jax.ShapeDtypeStruct((4, 3, 128, 128), BF16),
        compiler_params=params(10),
        name="line_sum",
    )(*terms)


def pack_kernel(place, *refs):
    terms, got, out = refs[:4], refs[4], refs[5]
    for s in range(4):
        mid = lax.rem(place[2] + 4 - s, 4)
        for t in range(2):
            half = jnp.where(place[0] == t, 0, 1)
            sums = [got[s, b] if t else added(terms, s, b) for b in range(3)]
            for q in range(2):
                tail = sums[2][:, 64 * q : 64 * q + 64]
                to = 4 * mid + 2 * half + q
                out[to, 0:128] = sums[q]
                out[to, 128:TOK] = jnp.concatenate([tail[:64], tail[64:]], axis=1)


def pack(place, terms, got):
    return pl.pallas_call(
        pack_kernel,
        in_specs=[SCALARS] + [WHOLE] * 5,
        out_specs=WHOLE,
        out_shape=jax.ShapeDtypeStruct((16, TOK, 128), BF16),
        compiler_params=params(10),
        name="pack",
    )(place, *terms, got)


def plane_sum_kernel(terms, out):
    value = terms[0].astype(F32)
    for j in range(1, 16):
        value = value + terms[j].astype(F32)
    fold = value[128:]
    out[0:128] = jnp.transpose(value[:128]).astype(BF16)
    tail = jnp.concatenate([fold[:, :64], fold[:, 64:]], axis=0)
    out[128:TOK] = jnp.transpose(tail).astype(BF16)


def plane_sum(terms):
    return pl.pallas_call(
        plane_sum_kernel,
        in_specs=[WHOLE],
        out_specs=WHOLE,
        out_shape=jax.ShapeDtypeStruct((TOK, 128), BF16),
        compiler_params=params(8),
        name="plane_sum",
    )(terms)


def outer_kernel(place, *refs):
    mine, others, p_own, p_other, out, held, right = refs[:4], refs[4:8], refs[8], refs[9], refs[10], refs[11], refs[12]
    i = pl.program_id(0)

    @pl.when(i == 0)
    def _():
        right[0:TOK] = p_own[...]
        right[TOK : 2 * TOK] = jnp.transpose(p_other[...].astype(F32)).astype(BF16)
        for d in range(4):
            for s, q in ORDER:
                rows = rows_at(place, d, s, q)
                held[rows.start // 128, 0:TOK] = mine[d][s, q]
                held[rows.start // 128, TOK : 2 * TOK] = others[d][s, q]

    left = jnp.concatenate([held[8 * i + j] for j in range(8)], axis=1)
    out[...] = lax.dot_general(left, right[...], (((0,), (0,)), ((), ())), preferred_element_type=F32).astype(BF16)


def outer(place, mine, others, p_own, p_other):
    rows = pl.BlockSpec((4, 2, TOK, 128), lambda i: (0, 0, 0, 0))
    whole = pl.BlockSpec((TOK, COLS), lambda i: (0, 0))
    turned = pl.BlockSpec((COLS, TOK), lambda i: (0, 0), pipeline_mode=pl.Buffered(1))
    return pl.pallas_call(
        outer_kernel,
        grid=(4,),
        in_specs=[SCALARS] + [rows] * 8 + [whole, turned],
        out_specs=pl.BlockSpec((1024, COLS), lambda i: (i, 0)),
        out_shape=jax.ShapeDtypeStruct((4096, COLS), BF16),
        scratch_shapes=[pltpu.VMEM((32, 2 * TOK, 128), BF16), pltpu.VMEM((2 * TOK, COLS), BF16)],
        compiler_params=params(16),
        cost_estimate=cost(4 * TOK * 4096 * COLS, 12 << 20),
        name="head_outer",
    )(place, *mine, *others, p_own, p_other)


def shards(hidden, tangent_hidden, head, tangent_head, allowed):
    k, v = lax.axis_index("dp"), lax.axis_index("vocab")
    z, y, x = v // 16, (v // 4) % 4, v % 4
    place = jnp.stack([k, jnp.where(k == 1, x, y), jnp.where(k == 1, y, x), z]).astype(jnp.int32)
    rows = join(*(pltpu.with_memory_space_constraint(h, pltpu.HBM) for h in (hidden, tangent_hidden)))
    both = arrange(place, [permute(rows, start_pairs(c)) for c in range(4)])
    middle = [both] + [permute(both, mid_shift(s)) for s in (1, 2, 3)]
    head, middle[1] = lax.optimization_barrier((head, middle[1]))
    head_near = load_near(head, "load_head")
    middle[2], head_near = lax.optimization_barrier((middle[2], head_near))
    own = jnp.stack([m[0] for m in middle])
    other = jnp.stack([m[1] for m in middle])
    other1, other3, own3 = permute(other, last_shift(1)), permute(other, last_shift(-1)), permute(own, last_shift(-1))
    other2 = permute(other1, last_shift(1))
    tangent_head, _ = lax.optimization_barrier((tangent_head, other1))
    near = (head_near, load_near(tangent_head, "load_tangent"))
    early = scores(place, (0, 1), [other, other1], *near, "other_first", 0)
    own, early = lax.optimization_barrier((own, early))
    own1, own2 = permute(own, last_shift(1)), permute(own3, last_shift(-1))
    owns, others = [own, own1, own2, own3], [other, other1, other2, other3]

    early = scores(place, (3,), [other3], *near, "other_next", 0, early)
    sent = scores(place, (2,), [other2], *near, "other_last", 10, early)
    got = permute(sent, swap_pairs())
    early = scores(place, (0, 3), [own, own3], *near, "own_first", 10)
    late = (got, jnp.transpose(allowed))
    early = scores(place, (1,), [own1], *near, "own_next", 0, early)
    weights, tangent, stats = scores(place, (2,), [own2], *near, "own_last", 0, early, late)
    every = lax.all_to_all(
        jnp.broadcast_to(stats[None], (64, 8, 128)), "vocab", split_axis=0, concat_axis=0, tiled=True
    )
    p_own, p_turned = make_product(every, stats, weights, tangent)
    p_other = permute(p_turned, swap_pairs())

    terms = back(place, p_turned, head_near, False, "back_own")
    mine = [terms[0]] + [permute(terms[d], last_shift(-d)) for d in (1, 3)]
    across = back(place, p_other, head_near, True, "back_other")
    theirs = [across[0]] + [permute(across[d], mid_shift(-d)) for d in (1, 3, 2)]
    term, _ = lax.optimization_barrier((terms[2], across[0]))
    mine.append(permute(term, last_shift(-2)))
    p_own, theirs[1] = lax.optimization_barrier((p_own, theirs[1]))
    head_product = outer(place, owns, others, p_own, p_other)
    head_product, theirs[0] = lax.optimization_barrier((head_product, theirs[0]))
    rest = permute(line_sum(theirs), swap_pairs())
    slab = pack(place, mine, rest)
    arrived = lax.all_to_all(slab, AXES, split_axis=0, concat_axis=0, tiled=True, axis_index_groups=plane_groups())
    hidden_product = plane_sum(arrived)
    return head_product, hidden_product


def solution(mesh):
    place = P("dp", "vocab")
    return jax.shard_map(shards, mesh=mesh, in_specs=(place,) * 5, out_specs=(place, place), check_vma=False)
```
